32 devices in a mesh: seq: 8 (over y, x, core), head: 4 (over z).
Axes of the slice: x: 2, y: 2, z: 4, core: 2. Of those that a mesh axis runs over, the one named last changes fastest.
Arguments:
- queries: bfloat16 [2, 2048, 20, 128], P(None, ('seq', 'head')), may hold values from -96 to 96
- grad_out: bfloat16 [2, 2048, 20, 128], P(None, ('seq', 'head')), may hold values from -6 to 6
- keys: bfloat16 [2048, 4, 128], P('seq', 'head'), may hold values from -6 to 6
- values: bfloat16 [2048, 4, 128], P('seq', 'head'), may hold values from -6 to 6
- doc_start: int32 [2048], replicated, may hold values from 0 to 2047, as said below
Outputs:
- query_grads: bfloat16 [2, 2048, 20, 128], P(None, ('seq', 'head'))
- key_grads: bfloat16 [2048, 4, 128], P('seq', 'head')
- value_grads: bfloat16 [2048, 4, 128], P('seq', 'head')
The draws below stay inside these ranges and needn't reach their ends.
Inputs may be any that keep to these rules, and one draw needn't show every extreme that they name: doc_start[i] is the first position of token i's document, so doc_start[i] <= i; it is 0 for every token before position 1024, at most four documents begin at or after it, and the last token begins a document of its own.
All inputs are finite; a program needn't handle non-finite values.
Results may differ from the reference program's by a relative error of at most 0.005.
Values may be sent and summed in bfloat16 or wider, within the bound.
No kernel may reach another device: no remote copies, remote signals or barrier semaphores. Data moves between devices by JAX's collectives and lax.ppermute only.
A program may use at most 128 MiB of HBM per device.

```python
import math
import jax
import jax.numpy as jnp
from jax import lax

H = 20
KVH = 4
DH = 128
L = 2
S = 2048


def draw_shared(key):
    base_key = jax.random.fold_in(key, 17)
    query_key, keys_key = jax.random.split(base_key, 2)
    key_rows = jax.random.normal(keys_key, (S, KVH, DH), jnp.float32)
    query_rows = jax.random.normal(query_key, (L, S, H, DH), jnp.float32)
    return (jnp.clip(query_rows, -96.0, 96.0), jnp.clip(key_rows, -6.0, 6.0))


def draw_queries(key, part):
    return draw_shared(key)[0].astype(jnp.bfloat16)


def draw_keys(key, part):
    return draw_shared(key)[1].astype(jnp.bfloat16)


def draw_doc_start(key, part):
    drawn = jax.random.randint(jax.random.fold_in(key, 29), (3,), S // 2, S - 1)
    starts = jnp.concatenate((drawn.astype(jnp.int32), jnp.full((1,), S - 1, jnp.int32)))
    positions = jnp.arange(S, dtype=jnp.int32)
    chosen = jnp.where(starts[None, :] <= positions[:, None], starts[None, :], 0)
    return jnp.max(chosen, axis=1).astype(jnp.int32)


def shard_levels(key, shape, cuts, smallest, top_value):
    def one(dim, shards_of):
        steps = jax.random.uniform(jax.random.fold_in(jax.random.fold_in(key, 6), dim), (shards_of,), jnp.float32, smallest / len(cuts), top_value / len(cuts))
        return jnp.repeat(jnp.exp(steps), shape[dim] // shards_of).reshape((-1,) + (1,) * (len(shape) - dim - 1))

    factor_of = one(*cuts[0])
    for cut in cuts[1:]:
        factor_of = factor_of * one(*cut)
    return factor_of


def gaussian(key, shape, deviation, reach, shards=(), kind=jnp.bfloat16):
    result = deviation * jax.random.normal(key, shape, jnp.float32)
    if shards:
        result = result * shard_levels(key, shape, shards, -0.22, 0.18)
    return jnp.clip(result, -reach, reach).astype(kind)


def setup_inputs(seed: int = 0) -> dict:
    arg_keys = jax.random.split(jax.random.key(seed), 6)
    queries = draw_queries(jax.random.fold_in(arg_keys[5], 71), 0)
    grad_out = gaussian(arg_keys[1], (L, S, H, DH), 1.0, 6.0, ((1, 32),))
    keys = draw_keys(jax.random.fold_in(arg_keys[5], 71), 0)
    values = gaussian(arg_keys[3], (S, KVH, DH), 1.0, 6.0, ((0, 8), (1, 4)))
    doc_start = draw_doc_start(jax.random.fold_in(arg_keys[5], 71), 0)
    return {"queries": queries, "grad_out": grad_out, "keys": keys, "values": values, "doc_start": doc_start}


def head_terms(query, grad, key_rows, value_rows, allowed, score_scale):
    scores = jnp.dot(query, key_rows.T, preferred_element_type=jnp.float32) * score_scale
    scores = jnp.where(allowed, scores, -jnp.inf)
    row_max = lax.optimization_barrier(jnp.max(scores, axis=1, keepdims=True))
    raw_weights = jnp.exp(scores - row_max)
    row_sum = lax.optimization_barrier(jnp.sum(raw_weights, axis=1, keepdims=True))
    grad_probs = jnp.dot(grad, value_rows.T, preferred_element_type=jnp.float32)
    row_delta = lax.optimization_barrier(jnp.sum(raw_weights * grad_probs, axis=1, keepdims=True)) / row_sum
    prob_rows = jnp.exp(scores - (row_max + jnp.log(row_sum)))
    grad_scores = prob_rows * (grad_probs - row_delta)
    grad_low = grad_scores.astype(jnp.bfloat16)
    prob_low = prob_rows.astype(jnp.bfloat16)
    query_part = (jnp.dot(grad_low, key_rows, preferred_element_type=jnp.float32) * score_scale).astype(jnp.bfloat16)
    key_part = jnp.dot(grad_low.T, query, preferred_element_type=jnp.float32)
    value_part = jnp.dot(prob_low.T, grad, preferred_element_type=jnp.float32)
    return (query_part, key_part, value_part)

def reference(queries, grad_out, keys, values, doc_start):
    positions = jnp.arange(S, dtype=jnp.int32)
    allowed = (positions[None, :] >= doc_start[:, None]) & (positions[None, :] <= positions[:, None])
    group_size = H // KVH
    score_scale = 1.0 / math.sqrt(DH)
    key_heads = jnp.repeat(jnp.moveaxis(keys, 1, 0), group_size, axis=0)
    value_heads = jnp.repeat(jnp.moveaxis(values, 1, 0), group_size, axis=0)
    layer_grads = []
    key_total = jnp.zeros((KVH, S, DH), jnp.float32)
    value_total = jnp.zeros((KVH, S, DH), jnp.float32)
    for layer_index in range(L):
        query_heads = jnp.moveaxis(queries[layer_index], 1, 0)
        grad_heads = jnp.moveaxis(grad_out[layer_index], 1, 0)
        query_part, key_part, value_part = lax.map(lambda packed: head_terms(packed[0], packed[1], packed[2], packed[3], allowed, score_scale), (query_heads, grad_heads, key_heads, value_heads))
        layer_grads.append(jnp.moveaxis(query_part, 0, 1))
        key_total = key_total + lax.optimization_barrier(jnp.sum(key_part.reshape(KVH, group_size, S, DH), axis=1))
        value_total = value_total + lax.optimization_barrier(jnp.sum(value_part.reshape(KVH, group_size, S, DH), axis=1))
    query_grads = jnp.stack(layer_grads, axis=0)
    key_grads = (jnp.moveaxis(key_total, 0, 1) * score_scale).astype(jnp.bfloat16)
    value_grads = jnp.moveaxis(value_total, 0, 1).astype(jnp.bfloat16)
    return (query_grads, key_grads, value_grads)
```

```python
import functools
import math

import jax
import jax.numpy as jnp
from jax import lax
from jax.experimental import pallas as pl
from jax.experimental.pallas import tpu as pltpu
from jax.sharding import PartitionSpec as P

NEG = -1e30
KEY_BLOCK = 256
VMEM_LIMIT = 56 * 1024 * 1024
SCORE_BYTES = 24 * 1024 * 1024


def exchange(x, seq_count, head_count, flip_seq, flip_head, sends=None):
    pairs = []
    for s in range(seq_count):
        for z in range(head_count):
            if sends is None or sends(s, z):
                pairs.append((s * head_count + z, (s ^ flip_seq) * head_count + (z ^ flip_head)))
    return lax.ppermute(x, ("seq", "head"), pairs)


def attention_kernel(
    column_count,
    head_group,
    info_ref,
    doc_ref,
    doc_rows_ref,
    *refs,
):
    chunk_refs = refs[:4]
    kv_refs = refs[4 : 4 + column_count]
    outs = refs[4 + column_count :]
    dq_refs = outs[:4]
    dkv_refs = outs[4 : 4 + column_count]
    (
        q_rows, g_rows, q_cols, g_cols, keys, values, keys_t,
        e_scr, d_scr, m_scr, max_scr, sum_scr, weight_scr, dqt, dk_acc, dv_acc,
    ) = outs[4 + column_count :]
    layers, group, tokens, width = chunk_refs[0].shape[1:]
    block_tokens = kv_refs[0].shape[2]
    total = keys.shape[0]
    pair = 2 * tokens
    row_count = 2 * pair
    scale = 1.0 / math.sqrt(width)
    exp_scale = scale * math.log2(math.e)
    column = info_ref[0]
    core = info_ref[1]
    z_pair = info_ref[2]
    z_bit = info_ref[3]

    for d in range(column_count):
        for b in range(2):
            start = pl.multiple_of(((column ^ d) * 2 + (core ^ b)) * block_tokens, block_tokens)
            keys[pl.ds(start, block_tokens), :] = kv_refs[d][b, 0]
            values[pl.ds(start, block_tokens), :] = kv_refs[d][b, 1]
    keys_t[...] = keys[...].T
    dk_acc[...] = jnp.zeros_like(dk_acc)
    dv_acc[...] = jnp.zeros_like(dv_acc)

    first = (column * 2 * block_tokens) + z_pair * pair
    second = first + block_tokens
    last = second + pair - 1
    low = doc_ref[first] // KEY_BLOCK
    high = last // KEY_BLOCK + 1
    open_from = doc_ref[last]
    starts, places = [], []
    for begin in (first, second):
        starts.append(doc_rows_ref[pl.ds(begin // pair, 1), :])
        places.append(begin + lax.broadcasted_iota(jnp.int32, (1, pair), 1))
    starts = jnp.concatenate(starts, axis=1)
    places = jnp.concatenate(places, axis=1)

    for layer in range(layers):
        for dz in range(2):
            for dc in range(2):
                at = pl.multiple_of(((core ^ dc) * 2 + (z_bit ^ dz)) * tokens, tokens)
                for h in range(group):
                    q_rows[h, pl.ds(at, tokens), :] = chunk_refs[2 * dz + dc][0, layer, h]
                    g_rows[h, pl.ds(at, tokens), :] = chunk_refs[2 * dz + dc][1, layer, h]
        for h in range(group):
            q_cols[:, pl.ds(h * row_count, row_count)] = q_rows[h].T
            g_cols[:, pl.ds(h * row_count, row_count)] = g_rows[h].T

        for base in range(0, group, head_group):
            heads = range(base, base + head_group)
            lanes = head_group * row_count
            left = base * row_count
            max_scr[...] = jnp.full_like(max_scr, NEG)
            sum_scr[...] = jnp.zeros_like(sum_scr)
            weight_scr[...] = jnp.zeros_like(weight_scr)

            def stats(j, _):
                key_start = pl.multiple_of(j * KEY_BLOCK, KEY_BLOCK)
                rows = pl.ds(key_start, KEY_BLOCK)
                key_block = keys[rows, :]
                value_block = values[rows, :]

                def run(masked):
                    if masked:
                        at = key_start + lax.broadcasted_iota(jnp.int32, (KEY_BLOCK, row_count), 0)
                        allowed = (at >= starts) & (at <= places)
                    for i, h in enumerate(heads):
                        cols = pl.ds(i * row_count, row_count)
                        scores = jnp.dot(
                            key_block, q_cols[:, pl.ds(h * row_count, row_count)],
                            preferred_element_type=jnp.float32,
                        )
                        grads = jnp.dot(
                            value_block, g_cols[:, pl.ds(h * row_count, row_count)],
                            preferred_element_type=jnp.float32,
                        )
                        if masked:
                            scores = jnp.where(allowed, scores, NEG)
                        old = max_scr[:, cols]
                        new = jnp.maximum(old, jnp.max(scores, axis=0, keepdims=True))
                        weights = jnp.exp2((scores - new) * exp_scale)
                        rescale = jnp.exp2((old - new) * exp_scale)
                        max_scr[:, cols] = new
                        m_scr[pl.ds(j, 1), cols] = new
                        sum_scr[:, cols] = sum_scr[:, cols] * rescale + jnp.sum(
                            weights, axis=0, keepdims=True
                        )
                        weight_scr[:, cols] = weight_scr[:, cols] * rescale + jnp.sum(
                            weights * grads, axis=0, keepdims=True
                        )
                        e_scr[rows, cols] = weights
                        d_scr[rows, cols] = grads

                whole = (key_start + KEY_BLOCK - 1 <= first) & (key_start >= open_from)

                @pl.when(whole)
                def _():
                    run(False)

                @pl.when(jnp.logical_not(whole))
                def _():
                    run(True)

                return 0

            lax.fori_loop(low, high, stats, 0)
            inverse = 1.0 / sum_scr[...]
            delta = weight_scr[...] * inverse
            weight_scr[...] = delta
            sum_scr[...] = inverse
            dqt[:, left : left + lanes] = jnp.zeros((width, lanes), jnp.float32)

            def grads_step(j, _):
                key_start = pl.multiple_of(j * KEY_BLOCK, KEY_BLOCK)
                rows = pl.ds(key_start, KEY_BLOCK)
                factor = jnp.exp2((m_scr[pl.ds(j, 1), :] - max_scr[...]) * exp_scale) * sum_scr[...]
                probs_parts, grad_parts = [], []
                for i, h in enumerate(heads):
                    cols = slice(i * row_count, (i + 1) * row_count)
                    probs = e_scr[rows, cols] * factor[:, cols]
                    grad_scores = probs * (d_scr[rows, cols] - weight_scr[:, cols])
                    probs_parts.append(probs.astype(jnp.bfloat16))
                    grad_parts.append(grad_scores.astype(jnp.bfloat16))
                probs_low = jnp.concatenate(probs_parts, axis=1)
                grad_low = jnp.concatenate(grad_parts, axis=1)
                g_all = g_rows[base : base + head_group].reshape(lanes, width)
                q_all = q_rows[base : base + head_group].reshape(lanes, width)
                dv_acc[rows, :] += jnp.dot(probs_low, g_all, preferred_element_type=jnp.float32)
                dk_acc[rows, :] += jnp.dot(grad_low, q_all, preferred_element_type=jnp.float32)
                dqt[:, left : left + lanes] += jnp.dot(
                    keys_t[:, rows], grad_low, preferred_element_type=jnp.float32
                )
                return 0

            lax.fori_loop(low, high, grads_step, 0)

        for h in range(group):
            q_rows[h] = (dqt[:, h * row_count : (h + 1) * row_count] * scale).T.astype(jnp.bfloat16)
        for dz in range(2):
            for dc in range(2):
                at = pl.multiple_of(((core ^ dc) * 2 + (z_bit ^ dz)) * tokens, tokens)
                for h in range(group):
                    dq_refs[2 * dz + dc][layer, h] = q_rows[h, pl.ds(at, tokens), :]

    for d in range(column_count):
        for b in range(2):
            start = pl.multiple_of(((column ^ d) * 2 + (core ^ b)) * block_tokens, block_tokens)
            rows = pl.ds(start, block_tokens)
            dkv_refs[d][b, 0] = (dk_acc[rows, :] * scale).astype(dkv_refs[d].dtype)
            dkv_refs[d][b, 1] = dv_acc[rows, :].astype(dkv_refs[d].dtype)


def attention(info, doc_start, chunks, kv_blocks):
    _, layers, group, tokens, width = chunks[0].shape
    column_count = len(kv_blocks)
    block_tokens = kv_blocks[0].shape[2]
    total = column_count * 2 * block_tokens
    row_count = 4 * tokens
    head_group = group
    while 8 * total * head_group * row_count > SCORE_BYTES:
        head_group = max(k for k in range(1, head_group) if group % k == 0)
    lanes = head_group * row_count
    smem = pl.BlockSpec(memory_space=pltpu.SMEM)
    vmem = pl.BlockSpec(memory_space=pltpu.VMEM)
    f32, bf16 = jnp.float32, jnp.bfloat16
    outs = [jax.ShapeDtypeStruct((layers, group, tokens, width), bf16)] * 4
    outs += [
        jax.ShapeDtypeStruct(kv_blocks[0].shape, f32 if d == 0 else bf16)
        for d in range(column_count)
    ]
    return pl.pallas_call(
        functools.partial(attention_kernel, column_count, head_group),
        out_shape=outs,
        in_specs=[smem, smem] + [vmem] * (1 + 4 + column_count),
        out_specs=[vmem] * len(outs),
        scratch_shapes=[
            pltpu.VMEM((group, row_count, width), bf16),
            pltpu.VMEM((group, row_count, width), bf16),
            pltpu.VMEM((width, group * row_count), bf16),
            pltpu.VMEM((width, group * row_count), bf16),
            pltpu.VMEM((total, width), bf16),
            pltpu.VMEM((total, width), bf16),
            pltpu.VMEM((width, total), bf16),
            pltpu.VMEM((total, lanes), f32),
            pltpu.VMEM((total, lanes), f32),
            pltpu.VMEM((total // KEY_BLOCK, lanes), f32),
            pltpu.VMEM((1, lanes), f32),
            pltpu.VMEM((1, lanes), f32),
            pltpu.VMEM((1, lanes), f32),
            pltpu.VMEM((width, group * row_count), f32),
            pltpu.VMEM((total, width), f32),
            pltpu.VMEM((total, width), f32),
        ],
        compiler_params=pltpu.CompilerParams(vmem_limit_bytes=VMEM_LIMIT),
        name="attention_backward",
    )(info, doc_start, doc_start.reshape(-1, 2 * tokens), *chunks, *kv_blocks)


def per_device(seq_count, head_count, queries, grad_out, keys, values, doc_start):
    layers, tokens, all_heads, width = queries.shape
    key_heads = head_count
    group = all_heads // key_heads
    column_count = seq_count // 2
    swap = functools.partial(exchange, seq_count=seq_count, head_count=head_count)
    s = lax.axis_index("seq")
    z = lax.axis_index("head")
    column, core = s // 2, s % 2
    z_pair, z_bit = z // 2, z % 2
    home = core == z_pair
    info = jnp.stack([column, core, z_pair, z_bit]).astype(jnp.int32)

    own = jnp.stack([keys[:, 0], values[:, 0]])
    from_far = swap(own, flip_seq=0, flip_head=2, sends=lambda s, z: s % 2 == z // 2)
    from_far_core = swap(own, flip_seq=1, flip_head=2, sends=lambda s, z: s % 2 != z // 2)
    from_core = swap(own, flip_seq=1, flip_head=0, sends=lambda s, z: s % 2 != z // 2)
    kv = jnp.stack([jnp.where(home, own, from_far), jnp.where(home, from_core, from_far_core)])
    kv_blocks = [kv] + [swap(kv, flip_seq=2 * d, flip_head=0) for d in range(1, column_count)]

    both = jnp.stack([queries, grad_out]).reshape(2, layers, tokens, 2, 2, group, width)
    both = jnp.transpose(both, (4, 3, 0, 1, 5, 2, 6))

    def piece(dz, dc):
        part = lax.dynamic_index_in_dim(both, z_bit ^ dz, 0, keepdims=False)
        return lax.dynamic_index_in_dim(part, core ^ dc, 0, keepdims=False)

    chunks = [
        piece(0, 0),
        swap(piece(0, 1), flip_seq=1, flip_head=0),
        swap(piece(1, 0), flip_seq=0, flip_head=1),
        swap(piece(1, 1), flip_seq=1, flip_head=1),
    ]
    results = attention(info, doc_start, chunks, kv_blocks)
    dq, dkv = results[:4], results[4:]

    back = [
        dq[0],
        swap(dq[1], flip_seq=1, flip_head=0),
        swap(dq[2], flip_seq=0, flip_head=1),
        swap(dq[3], flip_seq=1, flip_head=1),
    ]
    merged = jnp.stack(back).reshape(2, 2, layers, group, tokens, width)
    merged = jnp.where(z_bit == 1, merged[::-1], merged)
    merged = jnp.where(core == 1, merged[:, ::-1], merged)
    query_grads = jnp.transpose(merged, (2, 4, 1, 0, 3, 5)).reshape(
        layers, tokens, all_heads, width
    )

    mine = dkv[0]
    for d in range(1, column_count):
        mine = mine + swap(dkv[d], flip_seq=2 * d, flip_head=0).astype(jnp.float32)
    low = mine.astype(jnp.bfloat16)
    far = swap(low[0], flip_seq=0, flip_head=2, sends=lambda s, z: s % 2 != z // 2)
    far_core = swap(low[1], flip_seq=1, flip_head=2, sends=lambda s, z: s % 2 != z // 2)
    by_core = swap(low[1], flip_seq=1, flip_head=0, sends=lambda s, z: s % 2 == z // 2)
    near = jnp.where(home, mine[0], by_core.astype(jnp.float32))
    final = near + jnp.where(home, far, far_core).astype(jnp.float32)
    final = final.astype(jnp.bfloat16)[:, :, None, :]
    return query_grads, final[0], final[1]


def solution(mesh):
    tokens_spec = P(None, ("seq", "head"), None, None)
    keys_spec = P("seq", "head", None)
    return jax.shard_map(
        functools.partial(per_device, mesh.shape["seq"], mesh.shape["head"]),
        mesh=mesh,
        in_specs=(tokens_spec, tokens_spec, keys_spec, keys_spec, P()),
        out_specs=(tokens_spec, keys_spec, keys_spec),
        check_vma=False,
    )
```

```python
import functools
import math

import jax
import jax.numpy as jnp
from jax import lax
from jax.experimental import pallas as pl
from jax.experimental.pallas import tpu as pltpu
from jax.sharding import PartitionSpec as P

NEG = -1e30
KEY_BLOCK = 256
VMEM_LIMIT = 48 * 1024 * 1024
SCORE_BYTES = 24 * 1024 * 1024


def attention_kernel(column_count, group_lanes, info_ref, doc_ref, doc_rows_ref, *refs):
    chunk_refs = refs[:2]
    kv_refs = refs[2 : 2 + 2 * column_count]
    (
        dq_own, dq_send, kept_ref, sent_ref,
        q_rows, g_rows, q_cols, g_cols, keys, values,
        e_scr, d_scr, m_scr, max_scr, sum_scr, weight_scr, dqt, dk_acc, dv_acc,
    ) = refs[2 + 2 * column_count :]
    layers, group, tokens, width = dq_own.shape
    block_tokens = kv_refs[0].shape[1]
    pair = 2 * tokens
    heads = layers * group
    lanes = heads * pair
    wide = 2 * pair
    scale = 1.0 / math.sqrt(width)
    exp_scale = scale * math.log2(math.e)
    column = info_ref[0]
    core = info_ref[1]
    z_pair = info_ref[2]
    z_bit = info_ref[3]

    first = (column * 2 + core) * block_tokens + z_pair * pair
    last = first + pair - 1
    low = doc_ref[first] // KEY_BLOCK
    high = last // KEY_BLOCK + 1
    open_from = doc_ref[last]
    starts = doc_rows_ref[pl.ds(first // pair, 1), :]
    places = first + lax.broadcasted_iota(jnp.int32, (1, pair), 1)

    for d in range(column_count):
        for b in range(2):
            start = pl.multiple_of(((column ^ d) * 2 + (core ^ b)) * block_tokens, block_tokens)

            @pl.when((start <= last) & (start + block_tokens > low * KEY_BLOCK))
            def _():
                keys[pl.ds(start, block_tokens), :] = kv_refs[2 * d + b][0]
                values[pl.ds(start, block_tokens), :] = kv_refs[2 * d + b][1]

    dk_acc[...] = jnp.zeros_like(dk_acc)
    dv_acc[...] = jnp.zeros_like(dv_acc)
    for layer in range(layers):
        for h in range(group):
            n = layer * group + h
            for dz in range(2):
                at = pl.multiple_of((z_bit ^ dz) * tokens, tokens)
                q_rows[n, pl.ds(at, tokens), :] = chunk_refs[dz][0, layer, h]
                g_rows[n, pl.ds(at, tokens), :] = chunk_refs[dz][1, layer, h]
            q_cols[:, n * pair : (n + 1) * pair] = q_rows[n].T
            g_cols[:, n * pair : (n + 1) * pair] = g_rows[n].T

    for left in range(0, lanes, group_lanes):
        max_scr[...] = jnp.full_like(max_scr, NEG)
        sum_scr[...] = jnp.zeros_like(sum_scr)
        weight_scr[...] = jnp.zeros_like(weight_scr)

        def stats(j, _):
            key_start = pl.multiple_of(j * KEY_BLOCK, KEY_BLOCK)
            rows = pl.ds(key_start, KEY_BLOCK)
            key_block = keys[rows, :]
            value_block = values[rows, :]

            def run(masked):
                if masked:
                    at = key_start + lax.broadcasted_iota(jnp.int32, (KEY_BLOCK, pair), 0)
                    allowed = (at >= starts) & (at <= places)
                    allowed = jnp.concatenate([allowed, allowed], axis=1)
                for base in range(0, group_lanes, wide):
                    cols = slice(base, base + wide)
                    from_cols = slice(left + base, left + base + wide)
                    scores = jnp.dot(
                        key_block, q_cols[:, from_cols], preferred_element_type=jnp.float32
                    )
                    grads = jnp.dot(
                        value_block, g_cols[:, from_cols], preferred_element_type=jnp.float32
                    )
                    if masked:
                        scores = jnp.where(allowed, scores, NEG)
                    old = max_scr[:, cols]
                    new = jnp.maximum(old, jnp.max(scores, axis=0, keepdims=True))
                    weights = jnp.exp2((scores - new) * exp_scale)
                    rescale = jnp.exp2((old - new) * exp_scale)
                    max_scr[:, cols] = new
                    m_scr[pl.ds(j, 1), cols] = new
                    sum_scr[:, cols] = sum_scr[:, cols] * rescale + jnp.sum(
                        weights, axis=0, keepdims=True
                    )
                    weight_scr[:, cols] = weight_scr[:, cols] * rescale + jnp.sum(
                        weights * grads, axis=0, keepdims=True
                    )
                    e_scr[rows, cols] = weights
                    d_scr[rows, cols] = grads

            whole = (key_start + KEY_BLOCK - 1 <= first) & (key_start >= open_from)

            @pl.when(whole)
            def _():
                run(False)

            @pl.when(jnp.logical_not(whole))
            def _():
                run(True)

            return 0

        lax.fori_loop(low, high, stats, 0)
        inverse = 1.0 / sum_scr[...]
        weight_scr[...] = weight_scr[...] * inverse
        sum_scr[...] = inverse
        here = slice(left, left + group_lanes)
        dqt[:, here] = jnp.zeros((width, group_lanes), jnp.float32)

        def grads_step(j, _):
            key_start = pl.multiple_of(j * KEY_BLOCK, KEY_BLOCK)
            rows = pl.ds(key_start, KEY_BLOCK)
            factor = jnp.exp2((m_scr[pl.ds(j, 1), :] - max_scr[...]) * exp_scale) * sum_scr[...]
            probs_parts, grad_parts = [], []
            for base in range(0, group_lanes, wide):
                cols = slice(base, base + wide)
                probs = e_scr[rows, cols] * factor[:, cols]
                grad_scores = probs * (d_scr[rows, cols] - weight_scr[:, cols])
                probs_parts.append(probs.astype(jnp.bfloat16))
                grad_parts.append(grad_scores.astype(jnp.bfloat16))
            probs_low = jnp.concatenate(probs_parts, axis=1)
            grad_low = jnp.concatenate(grad_parts, axis=1)
            mine = slice(left // pair, (left + group_lanes) // pair)
            g_all = g_rows[mine].reshape(group_lanes, width)
            q_all = q_rows[mine].reshape(group_lanes, width)
            dv_acc[rows, :] += jnp.dot(probs_low, g_all, preferred_element_type=jnp.float32)
            dk_acc[rows, :] += jnp.dot(grad_low, q_all, preferred_element_type=jnp.float32)
            dqt[:, here] += jnp.dot(keys[rows, :].T, grad_low, preferred_element_type=jnp.float32)
            return 0

        lax.fori_loop(low, high, grads_step, 0)

    for n in range(heads):
        q_rows[n] = (dqt[:, n * pair : (n + 1) * pair] * scale).T.astype(jnp.bfloat16)
        for dz, out in enumerate((dq_own, dq_send)):
            at = pl.multiple_of((z_bit ^ dz) * tokens, tokens)
            out[n // group, n % group] = q_rows[n, pl.ds(at, tokens), :]

    for d in range(column_count):
        for b, out in enumerate((kept_ref, sent_ref)):
            start = pl.multiple_of(((column ^ d) * 2 + (core ^ b)) * block_tokens, block_tokens)
            rows = pl.ds(start, block_tokens)
            out[d, 0] = (dk_acc[rows, :] * scale).astype(out.dtype)
            out[d, 1] = dv_acc[rows, :].astype(out.dtype)


def attention(name, info, doc_start, chunks, kv_blocks):
    _, layers, group, tokens, width = chunks[0].shape
    column_count = len(kv_blocks) // 2
    block_tokens = kv_blocks[0].shape[1]
    total = column_count * 2 * block_tokens
    pair = 2 * tokens
    lanes = layers * group * pair
    wide = 2 * pair
    group_lanes = lanes
    while 8 * total * group_lanes > SCORE_BYTES and group_lanes > wide:
        group_lanes = max(k for k in range(wide, group_lanes, wide) if lanes % k == 0)
    smem = pl.BlockSpec(memory_space=pltpu.SMEM)
    vmem = pl.BlockSpec(memory_space=pltpu.VMEM)
    f32, bf16 = jnp.float32, jnp.bfloat16
    outs = [jax.ShapeDtypeStruct((layers, group, tokens, width), bf16)] * 2
    outs.append(jax.ShapeDtypeStruct((column_count, 2, block_tokens, width), f32))
    outs.append(jax.ShapeDtypeStruct((column_count, 2, block_tokens, width), bf16))
    return pl.pallas_call(
        functools.partial(attention_kernel, column_count, group_lanes),
        out_shape=outs,
        in_specs=[smem, smem] + [vmem] * (1 + 2 + 2 * column_count),
        out_specs=[vmem] * len(outs),
        scratch_shapes=[
            pltpu.VMEM((layers * group, pair, width), bf16),
            pltpu.VMEM((layers * group, pair, width), bf16),
            pltpu.VMEM((width, lanes), bf16),
            pltpu.VMEM((width, lanes), bf16),
            pltpu.VMEM((total, width), bf16),
            pltpu.VMEM((total, width), bf16),
            pltpu.VMEM((total, group_lanes), f32),
            pltpu.VMEM((total, group_lanes), f32),
            pltpu.VMEM((total // KEY_BLOCK, group_lanes), f32),
            pltpu.VMEM((1, group_lanes), f32),
            pltpu.VMEM((1, group_lanes), f32),
            pltpu.VMEM((1, group_lanes), f32),
            pltpu.VMEM((width, lanes), f32),
            pltpu.VMEM((total, width), f32),
            pltpu.VMEM((total, width), f32),
        ],
        compiler_params=pltpu.CompilerParams(vmem_limit_bytes=VMEM_LIMIT),
        name=name,
    )(info, doc_start, doc_start.reshape(-1, pair), *chunks, *kv_blocks)


def per_device(seq_count, head_count, queries, grad_out, keys, values, doc_start):
    layers, tokens, all_heads, width = queries.shape
    group = all_heads // head_count
    column_count = seq_count // 2
    columns = range(column_count)

    def swap(x, flip_seq, flip_head):
        pairs = [
            (s * head_count + z, (s ^ flip_seq) * head_count + (z ^ flip_head))
            for s in range(seq_count)
            for z in range(head_count)
        ]
        return lax.ppermute(x, ("seq", "head"), pairs)

    s = lax.axis_index("seq")
    z = lax.axis_index("head")
    info = jnp.stack([s // 2, s % 2, z // 2, z % 2]).astype(jnp.int32)

    own = jnp.stack([keys[:, 0], values[:, 0]])
    far_own = swap(own, 0, 2)
    near = [own] + [swap(own, 2 * d, 0) for d in columns[1:]]
    far = [far_own] + [swap(far_own, 2 * d, 0) for d in columns[1:]]
    near_blocks = [b for x in near for b in (x, swap(x, 1, 0))]
    far_blocks = [b for x in far for b in (x, swap(x, 1, 0))]

    both = jnp.stack([queries, grad_out]).reshape(2, layers, tokens, head_count, group, width)
    both = jnp.transpose(both, (3, 0, 1, 4, 2, 5))

    def piece(flip):
        return lax.dynamic_index_in_dim(both, z ^ flip, 0, keepdims=False)

    near_chunks = (piece(0), swap(piece(1), 0, 1))
    far_chunks = (piece(2), swap(piece(3), 0, 1))

    def finish(results):
        dq_own, dq_send, kept, sent = results
        dq_other = swap(dq_send, 0, 1)
        sums = kept + swap(sent, 1, 0).astype(jnp.float32)
        total = sums[0]
        for d in columns[1:]:
            total = total + swap(sums[d].astype(jnp.bfloat16), 2 * d, 0).astype(jnp.float32)
        return dq_own, dq_other, total

    near_dq, near_dq_other, near_total = finish(
        attention("attention_near", info, doc_start, near_chunks, near_blocks)
    )
    far_dq, far_dq_other, far_total = finish(
        attention("attention_far", info, doc_start, far_chunks, far_blocks)
    )

    pieces = jnp.stack([near_dq, near_dq_other, far_dq, far_dq_other])
    ordered = [
        lax.dynamic_index_in_dim(pieces, z ^ head, 0, keepdims=False) for head in range(head_count)
    ]
    query_grads = jnp.transpose(jnp.stack(ordered), (1, 3, 0, 2, 4))
    query_grads = query_grads.reshape(layers, tokens, all_heads, width)

    final = near_total + swap(far_total.astype(jnp.bfloat16), 0, 2).astype(jnp.float32)
    final = final.astype(jnp.bfloat16)[:, :, None, :]
    return query_grads, final[0], final[1]


def solution(mesh):
    tokens_spec = P(None, ("seq", "head"), None, None)
    keys_spec = P("seq", "head", None)
    return jax.shard_map(
        functools.partial(per_device, mesh.shape["seq"], mesh.shape["head"]),
        mesh=mesh,
        in_specs=(tokens_spec, tokens_spec, keys_spec, keys_spec, P()),
        out_specs=(tokens_spec, keys_spec, keys_spec),
        check_vma=False,
    )
```

```python
import functools
import math

import jax
import jax.numpy as jnp
from jax import lax
from jax.experimental import pallas as pl
from jax.experimental.pallas import tpu as pltpu
from jax.sharding import PartitionSpec as P

NEG = -1e30
KEY_BLOCK = 256
VMEM_LIMIT = 48 * 1024 * 1024
SCORE_BYTES = 24 * 1024 * 1024


def attention_kernel(column_count, group_lanes, merged, doc_ref, doc_rows_ref, *refs):
    chunk_refs = refs[:2]
    kv_refs = refs[2 : 2 + column_count]
    kv_other = refs[2 + column_count : 2 + 2 * column_count]
    if merged:
        kv_other = [refs[2 + column_count].at[d] for d in range(column_count)]
    (
        dq_own, dq_send, kept_ref, sent_ref,
        q_rows, g_rows, q_cols, g_cols, keys, values,
        e_scr, d_scr, m_scr, max_scr, sum_scr, weight_scr, dqt, dk_acc, dv_acc,
    ) = refs[-19:]
    layers, group, tokens, width = dq_own.shape
    block_tokens = kv_refs[0].shape[1]
    pair = 2 * tokens
    heads = layers * group
    lanes = heads * pair
    wide = 2 * pair
    scale = 1.0 / math.sqrt(width)
    exp_scale = scale * math.log2(math.e)
    s = lax.axis_index("seq")
    z = lax.axis_index("head")
    column, core, z_pair, z_bit = s // 2, s % 2, z // 2, z % 2

    first = (column * 2 + core) * block_tokens + z_pair * pair
    last = first + pair - 1
    low = doc_ref[first] // KEY_BLOCK
    high = last // KEY_BLOCK + 1
    open_from = doc_ref[last]
    starts = doc_rows_ref[pl.ds(first // pair, 1), :]
    places = first + lax.broadcasted_iota(jnp.int32, (1, pair), 1)

    for d in range(column_count):
        for b in range(2):
            start = pl.multiple_of(((column ^ d) * 2 + (core ^ b)) * block_tokens, block_tokens)

            @pl.when((start <= last) & (start + block_tokens > low * KEY_BLOCK))
            def _():
                block = kv_other[d] if b else kv_refs[d]
                keys[pl.ds(start, block_tokens), :] = block[0]
                values[pl.ds(start, block_tokens), :] = block[1]

    dk_acc[...] = jnp.zeros_like(dk_acc)
    dv_acc[...] = jnp.zeros_like(dv_acc)
    for layer in range(layers):
        for h in range(group):
            n = layer * group + h
            for dz in range(2):
                at = pl.multiple_of((z_bit ^ dz) * tokens, tokens)
                q_rows[n, pl.ds(at, tokens), :] = chunk_refs[dz][0, layer, h]
                g_rows[n, pl.ds(at, tokens), :] = chunk_refs[dz][1, layer, h]
            q_cols[:, n * pair : (n + 1) * pair] = q_rows[n].T
            g_cols[:, n * pair : (n + 1) * pair] = g_rows[n].T

    for left in range(0, lanes, group_lanes):
        max_scr[...] = jnp.full_like(max_scr, NEG)
        sum_scr[...] = jnp.zeros_like(sum_scr)
        weight_scr[...] = jnp.zeros_like(weight_scr)

        def stats(j, _):
            key_start = pl.multiple_of(j * KEY_BLOCK, KEY_BLOCK)
            rows = pl.ds(key_start, KEY_BLOCK)
            key_block = keys[rows, :]
            value_block = values[rows, :]

            def run(masked):
                if masked:
                    at = key_start + lax.broadcasted_iota(jnp.int32, (KEY_BLOCK, pair), 0)
                    allowed = (at >= starts) & (at <= places)
                    allowed = jnp.concatenate([allowed, allowed], axis=1)
                for base in range(0, group_lanes, wide):
                    cols = slice(base, base + wide)
                    from_cols = slice(left + base, left + base + wide)
                    scores = jnp.dot(
                        key_block, q_cols[:, from_cols], preferred_element_type=jnp.float32
                    )
                    grads = jnp.dot(
                        value_block, g_cols[:, from_cols], preferred_element_type=jnp.float32
                    )
                    if masked:
                        scores = jnp.where(allowed, scores, NEG)
                    old = max_scr[:, cols]
                    new = jnp.maximum(old, jnp.max(scores, axis=0, keepdims=True))
                    weights = jnp.exp2((scores - new) * exp_scale)
                    rescale = jnp.exp2((old - new) * exp_scale)
                    max_scr[:, cols] = new
                    m_scr[pl.ds(j, 1), cols] = new
                    sum_scr[:, cols] = sum_scr[:, cols] * rescale + jnp.sum(
                        weights, axis=0, keepdims=True
                    )
                    weight_scr[:, cols] = weight_scr[:, cols] * rescale + jnp.sum(
                        weights * grads, axis=0, keepdims=True
                    )
                    e_scr[rows, cols] = weights
                    d_scr[rows, cols] = grads

            whole = (key_start + KEY_BLOCK - 1 <= first) & (key_start >= open_from)

            @pl.when(whole)
            def _():
                run(False)

            @pl.when(jnp.logical_not(whole))
            def _():
                run(True)

            return 0

        lax.fori_loop(low, high, stats, 0)
        inverse = 1.0 / sum_scr[...]
        weight_scr[...] = weight_scr[...] * inverse
        sum_scr[...] = inverse
        here = slice(left, left + group_lanes)
        dqt[:, here] = jnp.zeros((width, group_lanes), jnp.float32)

        def grads_step(j, _):
            key_start = pl.multiple_of(j * KEY_BLOCK, KEY_BLOCK)
            rows = pl.ds(key_start, KEY_BLOCK)
            factor = jnp.exp2((m_scr[pl.ds(j, 1), :] - max_scr[...]) * exp_scale) * sum_scr[...]
            probs_parts, grad_parts = [], []
            for base in range(0, group_lanes, wide):
                cols = slice(base, base + wide)
                probs = e_scr[rows, cols] * factor[:, cols]
                grad_scores = probs * (d_scr[rows, cols] - weight_scr[:, cols])
                probs_parts.append(probs.astype(jnp.bfloat16))
                grad_parts.append(grad_scores.astype(jnp.bfloat16))
            probs_low = jnp.concatenate(probs_parts, axis=1)
            grad_low = jnp.concatenate(grad_parts, axis=1)
            mine = slice(left // pair, (left + group_lanes) // pair)
            g_all = g_rows[mine].reshape(group_lanes, width)
            q_all = q_rows[mine].reshape(group_lanes, width)
            dv_acc[rows, :] += jnp.dot(probs_low, g_all, preferred_element_type=jnp.float32)
            dk_acc[rows, :] += jnp.dot(grad_low, q_all, preferred_element_type=jnp.float32)
            dqt[:, here] += jnp.dot(keys[rows, :].T, grad_low, preferred_element_type=jnp.float32)
            return 0

        lax.fori_loop(low, high, grads_step, 0)

    for n in range(heads):
        q_rows[n] = (dqt[:, n * pair : (n + 1) * pair] * scale).T.astype(jnp.bfloat16)
        for dz, out in enumerate((dq_own, dq_send)):
            at = pl.multiple_of((z_bit ^ dz) * tokens, tokens)
            out[n // group, n % group] = q_rows[n, pl.ds(at, tokens), :]

    for d in range(column_count):
        for b, out in enumerate((kept_ref, sent_ref)):
            start = pl.multiple_of(((column ^ d) * 2 + (core ^ b)) * block_tokens, block_tokens)
            rows = pl.ds(start, block_tokens)
            out[d, 0] = (dk_acc[rows, :] * scale).astype(out.dtype)
            out[d, 1] = dv_acc[rows, :].astype(out.dtype)


def attention(name, doc_start, chunks, kv_own, kv_other, after=()):
    _, layers, group, tokens, width = chunks[0].shape
    column_count = len(kv_own)
    merged = len(kv_other) == 1
    block_tokens = kv_own[0].shape[1]
    total = column_count * 2 * block_tokens
    pair = 2 * tokens
    lanes = layers * group * pair
    wide = 2 * pair
    group_lanes = lanes
    while 8 * total * group_lanes > SCORE_BYTES and group_lanes > wide:
        group_lanes = max(k for k in range(wide, group_lanes, wide) if lanes % k == 0)
    smem = pl.BlockSpec(memory_space=pltpu.SMEM)
    vmem = pl.BlockSpec(memory_space=pltpu.VMEM)
    f32, bf16 = jnp.float32, jnp.bfloat16
    outs = [jax.ShapeDtypeStruct((layers, group, tokens, width), bf16)] * 2
    outs.append(jax.ShapeDtypeStruct((column_count, 2, block_tokens, width), f32))
    outs.append(jax.ShapeDtypeStruct((column_count, 2, block_tokens, width), bf16))
    return pl.pallas_call(
        functools.partial(attention_kernel, column_count, group_lanes, merged),
        out_shape=outs,
        in_specs=[smem] + [vmem] * (1 + 2 + column_count + len(kv_other))
        + [pl.BlockSpec(memory_space=pl.ANY)] * len(after),
        out_specs=[vmem] * len(outs),
        scratch_shapes=[
            pltpu.VMEM((layers * group, pair, width), bf16),
            pltpu.VMEM((layers * group, pair, width), bf16),
            pltpu.VMEM((width, lanes), bf16),
            pltpu.VMEM((width, lanes), bf16),
            pltpu.VMEM((total, width), bf16),
            pltpu.VMEM((total, width), bf16),
            pltpu.VMEM((total, group_lanes), f32),
            pltpu.VMEM((total, group_lanes), f32),
            pltpu.VMEM((total // KEY_BLOCK, group_lanes), f32),
            pltpu.VMEM((1, group_lanes), f32),
            pltpu.VMEM((1, group_lanes), f32),
            pltpu.VMEM((1, group_lanes), f32),
            pltpu.VMEM((width, lanes), f32),
            pltpu.VMEM((total, width), f32),
            pltpu.VMEM((total, width), f32),
        ],
        compiler_params=pltpu.CompilerParams(vmem_limit_bytes=VMEM_LIMIT),
        cost_estimate=pl.CostEstimate(
            flops=10 * lanes * total * width,
            bytes_accessed=16 * total * width,
            transcendentals=lanes * total,
        ),
        name=name,
    )(doc_start, doc_start.reshape(-1, pair), *chunks, *kv_own, *kv_other, *after)


def per_device(seq_count, head_count, queries, grad_out, keys, values, doc_start):
    layers, tokens, all_heads, width = queries.shape
    group = all_heads // head_count
    column_count = seq_count // 2
    columns = range(column_count)

    def swap(x, flip_seq, flip_head):
        pairs = [
            (s * head_count + z, (s ^ flip_seq) * head_count + (z ^ flip_head))
            for s in range(seq_count)
            for z in range(head_count)
        ]
        return lax.ppermute(x, ("seq", "head"), pairs)

    z = lax.axis_index("head")

    own = jnp.stack([keys[:, 0], values[:, 0]])
    far_own = swap(own, 0, 2)
    near = [own] + [swap(own, 2 * d, 0) for d in columns[1:]]
    far = [far_own] + [swap(far_own, 2 * d, 0) for d in columns[1:]]
    near_other = [swap(jnp.stack(near), 1, 0)]
    far_other = [swap(x, 1, 0) for x in far]

    both = jnp.stack([queries, grad_out]).reshape(2, layers, tokens, head_count, group, width)
    both = jnp.transpose(both, (3, 0, 1, 4, 2, 5))

    def piece(flip):
        return lax.dynamic_index_in_dim(both, z ^ flip, 0, keepdims=False)

    near_chunks = (piece(0), swap(piece(1), 0, 1))
    far_chunks = (piece(2), swap(piece(3), 0, 1))

    near_dq, near_dq_send, near_kept, near_sent = attention(
        "attention_near", doc_start, near_chunks, near, near_other
    )
    far_dq, far_dq_send, far_kept, far_sent = attention(
        "attention_far", doc_start, far_chunks, far, far_other
    )

    def add_cores(kept, sent):
        sums = kept + swap(sent, 1, 0).astype(jnp.float32)
        return sums[0], [sums[d].astype(jnp.bfloat16) for d in columns[1:]]

    def add_columns(mine, parts):
        for d, part in zip(columns[1:], parts):
            mine = mine + swap(part, 2 * d, 0).astype(jnp.float32)
        return mine

    far_total = add_columns(*add_cores(far_kept, far_sent))
    far_low = far_total.astype(jnp.bfloat16)
    near_total = add_columns(*add_cores(near_kept, near_sent))
    final = near_total + swap(far_low, 0, 2).astype(jnp.float32)
    final = final.astype(jnp.bfloat16)[:, :, None, :]

    pieces = jnp.stack([near_dq, swap(near_dq_send, 0, 1), far_dq, swap(far_dq_send, 0, 1)])
    ordered = [
        lax.dynamic_index_in_dim(pieces, z ^ head, 0, keepdims=False) for head in range(head_count)
    ]
    query_grads = jnp.transpose(jnp.stack(ordered), (1, 3, 0, 2, 4))
    query_grads = query_grads.reshape(layers, tokens, all_heads, width)
    return query_grads, final[0], final[1]


def solution(mesh):
    tokens_spec = P(None, ("seq", "head"), None, None)
    keys_spec = P("seq", "head", None)
    return jax.shard_map(
        functools.partial(per_device, mesh.shape["seq"], mesh.shape["head"]),
        mesh=mesh,
        in_specs=(tokens_spec, tokens_spec, keys_spec, keys_spec, P()),
        out_specs=(tokens_spec, keys_spec, keys_spec),
        check_vma=False,
    )
```

```python
import functools
import math

import jax
import jax.numpy as jnp
from jax import lax
from jax.experimental import pallas as pl
from jax.experimental.pallas import tpu as pltpu
from jax.sharding import PartitionSpec as P

NEG = -1e30
KEY_BLOCK = 256
VMEM_LIMIT = 48 * 1024 * 1024
SCORE_BYTES = 24 * 1024 * 1024


def attention_kernel(column_count, group_lanes, merged, doc_ref, doc_rows_ref, *refs):
    chunk_refs = refs[:2]
    kv_refs = refs[2 : 2 + column_count]
    kv_other = refs[2 + column_count : 2 + 2 * column_count]
    if merged:
        kv_other = [refs[2 + column_count].at[d] for d in range(column_count)]
    (
        dq_own, dq_send, kept_ref, sent_ref,
        q_rows, g_rows, q_cols, g_cols, keys, values,
        e_scr, d_scr, m_scr, max_scr, sum_scr, weight_scr, dqt, dk_acc, dv_acc,
    ) = refs[-19:]
    layers, group, tokens, width = dq_own.shape
    block_tokens = kv_refs[0].shape[1]
    pair = 2 * tokens
    heads = layers * group
    lanes = heads * pair
    wide = 2 * pair
    scale = 1.0 / math.sqrt(width)
    exp_scale = scale * math.log2(math.e)
    s = lax.axis_index("seq")
    z = lax.axis_index("head")
    column, core, z_pair, z_bit = s // 2, s % 2, z // 2, z % 2

    first = (column * 2 + core) * block_tokens + z_pair * pair
    last = first + pair - 1
    low = doc_ref[first] // KEY_BLOCK
    high = last // KEY_BLOCK + 1
    open_from = doc_ref[last]
    starts = doc_rows_ref[pl.ds(first // pair, 1), :]
    places = first + lax.broadcasted_iota(jnp.int32, (1, pair), 1)

    for d in range(column_count):
        for b in range(2):
            start = pl.multiple_of(((column ^ d) * 2 + (core ^ b)) * block_tokens, block_tokens)

            @pl.when((start <= last) & (start + block_tokens > low * KEY_BLOCK))
            def _():
                block = kv_other[d] if b else kv_refs[d]
                keys[pl.ds(start, block_tokens), :] = block[0]
                values[pl.ds(start, block_tokens), :] = block[1]

    if group_lanes != lanes:
        dk_acc[...] = jnp.zeros_like(dk_acc)
        dv_acc[...] = jnp.zeros_like(dv_acc)
    for layer in range(layers):
        for h in range(group):
            n = layer * group + h
            for dz in range(2):
                at = pl.multiple_of((z_bit ^ dz) * tokens, tokens)
                q_rows[n, pl.ds(at, tokens), :] = chunk_refs[dz][0, layer, h]
                g_rows[n, pl.ds(at, tokens), :] = chunk_refs[dz][1, layer, h]
            q_cols[:, n * pair : (n + 1) * pair] = q_rows[n].T
            g_cols[:, n * pair : (n + 1) * pair] = g_rows[n].T

    def over_keys(step):
        def two(i, _):
            step(low + 2 * i, 2 * KEY_BLOCK)
            return 0

        lax.fori_loop(0, (high - low) // 2, two, 0)

        @pl.when((high - low) % 2 == 1)
        def _():
            step(high - 1, KEY_BLOCK)

    for left in range(0, lanes, group_lanes):
        max_scr[...] = jnp.full_like(max_scr, NEG)
        sum_scr[...] = jnp.zeros_like(sum_scr)
        weight_scr[...] = jnp.zeros_like(weight_scr)

        def stats(j, size):
            key_start = pl.multiple_of(j * KEY_BLOCK, KEY_BLOCK)
            rows = pl.ds(key_start, size)
            key_block = keys[rows, :]
            value_block = values[rows, :]

            def run(masked):
                if masked:
                    at = key_start + lax.broadcasted_iota(jnp.int32, (size, pair), 0)
                    allowed = (at >= starts) & (at <= places)
                    allowed = jnp.concatenate([allowed, allowed], axis=1)
                news = []
                for base in range(0, group_lanes, wide):
                    cols = slice(base, base + wide)
                    from_cols = slice(left + base, left + base + wide)
                    scores = jnp.dot(
                        key_block, q_cols[:, from_cols], preferred_element_type=jnp.float32
                    )
                    if masked:
                        scores = jnp.where(allowed, scores, NEG)
                    e_scr[rows, cols] = scores
                    news.append(jnp.maximum(max_scr[:, cols], jnp.max(scores, axis=0, keepdims=True)))
                for base in range(0, group_lanes, wide):
                    cols = slice(base, base + wide)
                    from_cols = slice(left + base, left + base + wide)
                    grads = jnp.dot(
                        value_block, g_cols[:, from_cols], preferred_element_type=jnp.float32
                    )
                    old, new = max_scr[:, cols], news[base // wide]
                    weights = jnp.exp2((e_scr[rows, cols] - new) * exp_scale)
                    rescale = jnp.exp2((old - new) * exp_scale)
                    max_scr[:, cols] = new
                    m_scr[pl.ds(j, 1), cols] = new
                    sum_scr[:, cols] = sum_scr[:, cols] * rescale + jnp.sum(
                        weights, axis=0, keepdims=True
                    )
                    weight_scr[:, cols] = weight_scr[:, cols] * rescale + jnp.sum(
                        weights * grads, axis=0, keepdims=True
                    )
                    e_scr[rows, cols] = weights
                    d_scr[rows, cols] = grads

            whole = (key_start + size - 1 <= first) & (key_start >= open_from)

            @pl.when(whole)
            def _():
                run(False)

            @pl.when(jnp.logical_not(whole))
            def _():
                run(True)

        over_keys(stats)
        inverse = 1.0 / sum_scr[...]
        weight_scr[...] = weight_scr[...] * inverse
        sum_scr[...] = inverse
        here = slice(left, left + group_lanes)
        dqt[:, here] = jnp.zeros((width, group_lanes), jnp.float32)

        def grads_step(j, size):
            key_start = pl.multiple_of(j * KEY_BLOCK, KEY_BLOCK)
            rows = pl.ds(key_start, size)
            factor = jnp.exp2((m_scr[pl.ds(j, 1), :] - max_scr[...]) * exp_scale) * sum_scr[...]
            probs_parts, grad_parts = [], []
            for base in range(0, group_lanes, wide):
                cols = slice(base, base + wide)
                probs = e_scr[rows, cols] * factor[:, cols]
                grad_scores = probs * (d_scr[rows, cols] - weight_scr[:, cols])
                probs_parts.append(probs.astype(jnp.bfloat16))
                grad_parts.append(grad_scores.astype(jnp.bfloat16))
            probs_low = jnp.concatenate(probs_parts, axis=1)
            grad_low = jnp.concatenate(grad_parts, axis=1)
            mine = slice(left // pair, (left + group_lanes) // pair)
            g_all = g_rows[mine].reshape(group_lanes, width)
            q_all = q_rows[mine].reshape(group_lanes, width)
            dv_part = jnp.dot(probs_low, g_all, preferred_element_type=jnp.float32)
            dk_part = jnp.dot(grad_low, q_all, preferred_element_type=jnp.float32)
            if group_lanes == lanes:
                dv_acc[rows, :] = dv_part
                dk_acc[rows, :] = dk_part
            else:
                dv_acc[rows, :] += dv_part
                dk_acc[rows, :] += dk_part
            dqt[:, here] += jnp.dot(keys[rows, :].T, grad_low, preferred_element_type=jnp.float32)

        over_keys(grads_step)

    for n in range(heads):
        q_rows[n] = (dqt[:, n * pair : (n + 1) * pair] * scale).T.astype(jnp.bfloat16)
        for dz, out in enumerate((dq_own, dq_send)):
            at = pl.multiple_of((z_bit ^ dz) * tokens, tokens)
            out[n // group, n % group] = q_rows[n, pl.ds(at, tokens), :]

    for d in range(column_count):
        for b, out in enumerate((kept_ref, sent_ref)):
            start = pl.multiple_of(((column ^ d) * 2 + (core ^ b)) * block_tokens, block_tokens)
            rows = pl.ds(start, block_tokens)
            seen = (start >= low * KEY_BLOCK) & (start < high * KEY_BLOCK)

            @pl.when(seen)
            def _():
                out[d, 0] = (dk_acc[rows, :] * scale).astype(out.dtype)
                out[d, 1] = dv_acc[rows, :].astype(out.dtype)

            @pl.when(jnp.logical_not(seen))
            def _():
                out[d] = jnp.zeros(out.shape[1:], out.dtype)


def attention(name, doc_start, chunks, kv_own, kv_other, after=()):
    _, layers, group, tokens, width = chunks[0].shape
    column_count = len(kv_own)
    merged = len(kv_other) == 1
    block_tokens = kv_own[0].shape[1]
    total = column_count * 2 * block_tokens
    pair = 2 * tokens
    lanes = layers * group * pair
    wide = 2 * pair
    group_lanes = lanes
    while 8 * total * group_lanes > SCORE_BYTES and group_lanes > wide:
        group_lanes = max(k for k in range(wide, group_lanes, wide) if lanes % k == 0)
    smem = pl.BlockSpec(memory_space=pltpu.SMEM)
    vmem = pl.BlockSpec(memory_space=pltpu.VMEM)
    f32, bf16 = jnp.float32, jnp.bfloat16
    outs = [jax.ShapeDtypeStruct((layers, group, tokens, width), bf16)] * 2
    outs.append(jax.ShapeDtypeStruct((column_count, 2, block_tokens, width), f32))
    outs.append(jax.ShapeDtypeStruct((column_count, 2, block_tokens, width), bf16))
    return pl.pallas_call(
        functools.partial(attention_kernel, column_count, group_lanes, merged),
        out_shape=outs,
        in_specs=[smem] + [vmem] * (1 + 2 + column_count + len(kv_other))
        + [pl.BlockSpec(memory_space=pl.ANY)] * len(after),
        out_specs=[vmem] * len(outs),
        scratch_shapes=[
            pltpu.VMEM((layers * group, pair, width), bf16),
            pltpu.VMEM((layers * group, pair, width), bf16),
            pltpu.VMEM((width, lanes), bf16),
            pltpu.VMEM((width, lanes), bf16),
            pltpu.VMEM((total, width), bf16),
            pltpu.VMEM((total, width), bf16),
            pltpu.VMEM((total, group_lanes), f32),
            pltpu.VMEM((total, group_lanes), f32),
            pltpu.VMEM((total // KEY_BLOCK, group_lanes), f32),
            pltpu.VMEM((1, group_lanes), f32),
            pltpu.VMEM((1, group_lanes), f32),
            pltpu.VMEM((1, group_lanes), f32),
            pltpu.VMEM((width, lanes), f32),
            pltpu.VMEM((total, width), f32),
            pltpu.VMEM((total, width), f32),
        ],
        compiler_params=pltpu.CompilerParams(vmem_limit_bytes=VMEM_LIMIT),
        cost_estimate=pl.CostEstimate(
            flops=10 * lanes * total * width,
            bytes_accessed=16 * total * width,
            transcendentals=lanes * total,
        ),
        name=name,
    )(doc_start, doc_start.reshape(-1, pair), *chunks, *kv_own, *kv_other, *after)


def per_device(seq_count, head_count, queries, grad_out, keys, values, doc_start):
    layers, tokens, all_heads, width = queries.shape
    group = all_heads // head_count
    column_count = seq_count // 2
    columns = range(column_count)

    def swap(x, flip_seq, flip_head):
        pairs = [
            (s * head_count + z, (s ^ flip_seq) * head_count + (z ^ flip_head))
            for s in range(seq_count)
            for z in range(head_count)
        ]
        return lax.ppermute(x, ("seq", "head"), pairs)

    z = lax.axis_index("head")

    own = jnp.stack([keys[:, 0], values[:, 0]])
    far_own = swap(own, 0, 2)
    near = [own] + [swap(own, 2 * d, 0) for d in columns[1:]]
    far = [far_own] + [swap(far_own, 2 * d, 0) for d in columns[1:]]
    near_other = [swap(jnp.stack(near), 1, 0)]
    far_other = [swap(x, 1, 0) for x in far]

    both = jnp.stack([queries, grad_out]).reshape(2, layers, tokens, head_count, group, width)
    both = jnp.transpose(both, (3, 0, 1, 4, 2, 5))

    def piece(flip):
        return lax.dynamic_index_in_dim(both, z ^ flip, 0, keepdims=False)

    near_chunks = (piece(0), swap(piece(1), 0, 1))
    far_chunks = (piece(2), swap(piece(3), 0, 1))

    near_dq, near_dq_send, near_kept, near_sent = attention(
        "attention_near", doc_start, near_chunks, near, near_other
    )
    far_dq, far_dq_send, far_kept, far_sent = attention(
        "attention_far", doc_start, far_chunks, far, far_other
    )

    def add_cores(kept, sent):
        sums = kept + swap(sent, 1, 0).astype(jnp.float32)
        return sums[0], [sums[d].astype(jnp.bfloat16) for d in columns[1:]]

    def add_columns(mine, parts):
        for d, part in zip(columns[1:], parts):
            mine = mine + swap(part, 2 * d, 0).astype(jnp.float32)
        return mine

    far_total = add_columns(*add_cores(far_kept, far_sent))
    far_low = far_total.astype(jnp.bfloat16)
    near_total = add_columns(*add_cores(near_kept, near_sent))
    final = near_total + swap(far_low, 0, 2).astype(jnp.float32)
    final = final.astype(jnp.bfloat16)[:, :, None, :]

    pieces = jnp.stack([near_dq, swap(near_dq_send, 0, 1), far_dq, swap(far_dq_send, 0, 1)])
    ordered = [
        lax.dynamic_index_in_dim(pieces, z ^ head, 0, keepdims=False) for head in range(head_count)
    ]
    query_grads = jnp.transpose(jnp.stack(ordered), (1, 3, 0, 2, 4))
    query_grads = query_grads.reshape(layers, tokens, all_heads, width)
    return query_grads, final[0], final[1]


def solution(mesh):
    tokens_spec = P(None, ("seq", "head"), None, None)
    keys_spec = P("seq", "head", None)
    return jax.shard_map(
        functools.partial(per_device, mesh.shape["seq"], mesh.shape["head"]),
        mesh=mesh,
        in_specs=(tokens_spec, tokens_spec, keys_spec, keys_spec, P()),
        out_specs=(tokens_spec, keys_spec, keys_spec),
        check_vma=False,
    )
```

```python
import functools
import math

import jax
import jax.numpy as jnp
from jax import lax
from jax.experimental import pallas as pl
from jax.experimental.pallas import tpu as pltpu
from jax.sharding import PartitionSpec as P

NEG = -1e30
KEY_BLOCK = 256
VMEM_LIMIT = 48 * 1024 * 1024
SCORE_BYTES = 24 * 1024 * 1024


def attention_kernel(column_count, group_lanes, merged, doc_ref, doc_rows_ref, *refs):
    chunk_refs = refs[:2]
    kv_refs = refs[2 : 2 + column_count]
    kv_other = refs[2 + column_count : 2 + 2 * column_count]
    if merged:
        kv_other = [refs[2 + column_count].at[d] for d in range(column_count)]
    (
        dq_own, dq_send, kept_ref, sent_ref,
        q_rows, g_rows, q_cols, g_cols, keys, values,
        e_scr, d_scr, m_scr, max_scr, sum_scr, weight_scr, dqt, dk_acc, dv_acc,
    ) = refs[-19:]
    layers, group, tokens, width = dq_own.shape
    block_tokens = kv_refs[0].shape[1]
    pair = 2 * tokens
    heads = layers * group
    lanes = heads * pair
    wide = 2 * pair
    scale = 1.0 / math.sqrt(width)
    exp_scale = scale * math.log2(math.e)
    s = lax.axis_index("seq")
    z = lax.axis_index("head")
    column, core, z_pair, z_bit = s // 2, s % 2, z // 2, z % 2

    first = (column * 2 + core) * block_tokens + z_pair * pair
    last = first + pair - 1
    low = doc_ref[first] // KEY_BLOCK
    high = last // KEY_BLOCK + 1
    open_from = doc_ref[last]
    starts = doc_rows_ref[pl.ds(first // pair, 1), :]
    places = first + lax.broadcasted_iota(jnp.int32, (1, pair), 1)

    for d in range(column_count):
        for b in range(2):
            start = pl.multiple_of(((column ^ d) * 2 + (core ^ b)) * block_tokens, block_tokens)

            @pl.when((start <= last) & (start + block_tokens > low * KEY_BLOCK))
            def _():
                block = kv_other[d] if b else kv_refs[d]
                keys[pl.ds(start, block_tokens), :] = block[0]
                values[pl.ds(start, block_tokens), :] = block[1]

    if group_lanes != lanes:
        dk_acc[...] = jnp.zeros_like(dk_acc)
        dv_acc[...] = jnp.zeros_like(dv_acc)
    for layer in range(layers):
        for h in range(group):
            n = layer * group + h
            for dz in range(2):
                at = pl.multiple_of((z_bit ^ dz) * tokens, tokens)
                q_rows[n, pl.ds(at, tokens), :] = chunk_refs[dz][0, layer, h]
                g_rows[n, pl.ds(at, tokens), :] = chunk_refs[dz][1, layer, h]
            q_cols[:, n * pair : (n + 1) * pair] = q_rows[n].T
            g_cols[:, n * pair : (n + 1) * pair] = g_rows[n].T

    def over_keys(step):
        def two(i, _):
            step(low + 2 * i, 2 * KEY_BLOCK)
            return 0

        lax.fori_loop(0, (high - low) // 2, two, 0)

        @pl.when((high - low) % 2 == 1)
        def _():
            step(high - 1, KEY_BLOCK)

    for left in range(0, lanes, group_lanes):
        max_scr[...] = jnp.full_like(max_scr, NEG)
        sum_scr[...] = jnp.zeros_like(sum_scr)
        weight_scr[...] = jnp.zeros_like(weight_scr)

        def stats(j, size):
            key_start = pl.multiple_of(j * KEY_BLOCK, KEY_BLOCK)
            rows = pl.ds(key_start, size)
            key_block = keys[rows, :]
            value_block = values[rows, :]

            def run(masked):
                if masked:
                    at = key_start + lax.broadcasted_iota(jnp.int32, (size, pair), 0)
                    allowed = (at >= starts) & (at <= places)
                    allowed = jnp.concatenate([allowed, allowed], axis=1)
                news = []
                for base in range(0, group_lanes, wide):
                    cols = slice(base, base + wide)
                    from_cols = slice(left + base, left + base + wide)
                    scores = jnp.dot(
                        key_block, q_cols[:, from_cols], preferred_element_type=jnp.float32
                    )
                    if masked:
                        scores = jnp.where(allowed, scores, NEG)
                    e_scr[rows, cols] = scores
                    news.append(jnp.maximum(max_scr[:, cols], jnp.max(scores, axis=0, keepdims=True)))
                for base in range(0, group_lanes, wide):
                    cols = slice(base, base + wide)
                    from_cols = slice(left + base, left + base + wide)
                    grads = jnp.dot(
                        value_block, g_cols[:, from_cols], preferred_element_type=jnp.float32
                    )
                    old, new = max_scr[:, cols], news[base // wide]
                    weights = jnp.exp2((e_scr[rows, cols] - new) * exp_scale)
                    rescale = jnp.exp2((old - new) * exp_scale)
                    max_scr[:, cols] = new
                    m_scr[pl.ds(j, 1), cols] = new
                    sum_scr[:, cols] = sum_scr[:, cols] * rescale + jnp.sum(
                        weights, axis=0, keepdims=True
                    )
                    weight_scr[:, cols] = weight_scr[:, cols] * rescale + jnp.sum(
                        weights * grads, axis=0, keepdims=True
                    )
                    e_scr[rows, cols] = weights
                    d_scr[rows, cols] = grads

            whole = (key_start + size - 1 <= first) & (key_start >= open_from)

            @pl.when(whole)
            def _():
                run(False)

            @pl.when(jnp.logical_not(whole))
            def _():
                run(True)

        over_keys(stats)
        inverse = 1.0 / sum_scr[...]
        weight_scr[...] = weight_scr[...] * inverse
        sum_scr[...] = inverse
        here = slice(left, left + group_lanes)
        dqt[:, here] = jnp.zeros((width, group_lanes), jnp.float32)

        def grads_step(j, size):
            key_start = pl.multiple_of(j * KEY_BLOCK, KEY_BLOCK)
            rows = pl.ds(key_start, size)
            factor = jnp.exp2((m_scr[pl.ds(j, 1), :] - max_scr[...]) * exp_scale) * sum_scr[...]
            probs_parts, grad_parts = [], []
            for base in range(0, group_lanes, wide):
                cols = slice(base, base + wide)
                probs = e_scr[rows, cols] * factor[:, cols]
                grad_scores = probs * (d_scr[rows, cols] - weight_scr[:, cols])
                probs_parts.append(probs.astype(jnp.bfloat16))
                grad_parts.append(grad_scores.astype(jnp.bfloat16))
            probs_low = jnp.concatenate(probs_parts, axis=1)
            grad_low = jnp.concatenate(grad_parts, axis=1)
            mine = slice(left // pair, (left + group_lanes) // pair)
            g_all = g_rows[mine].reshape(group_lanes, width)
            q_all = q_rows[mine].reshape(group_lanes, width)
            dv_part = jnp.dot(probs_low, g_all, preferred_element_type=jnp.float32)
            dk_part = jnp.dot(grad_low, q_all, preferred_element_type=jnp.float32)
            if group_lanes == lanes:
                dv_acc[rows, :] = dv_part
                dk_acc[rows, :] = dk_part
            else:
                dv_acc[rows, :] += dv_part
                dk_acc[rows, :] += dk_part
            dqt[:, here] += jnp.dot(keys[rows, :].T, grad_low, preferred_element_type=jnp.float32)

        over_keys(grads_step)

    for n in range(heads):
        q_rows[n] = (dqt[:, n * pair : (n + 1) * pair] * scale).T.astype(jnp.bfloat16)
        for dz, out in enumerate((dq_own, dq_send)):
            at = pl.multiple_of((z_bit ^ dz) * tokens, tokens)
            out[n // group, n % group] = q_rows[n, pl.ds(at, tokens), :]

    for d in range(column_count):
        for b, out in enumerate((kept_ref, sent_ref)):
            start = pl.multiple_of(((column ^ d) * 2 + (core ^ b)) * block_tokens, block_tokens)
            rows = pl.ds(start, block_tokens)
            seen = (start >= low * KEY_BLOCK) & (start < high * KEY_BLOCK)

            @pl.when(seen)
            def _():
                out[d, 0] = (dk_acc[rows, :] * scale).astype(out.dtype)
                out[d, 1] = dv_acc[rows, :].astype(out.dtype)

            @pl.when(jnp.logical_not(seen))
            def _():
                out[d] = jnp.zeros(out.shape[1:], out.dtype)


def attention(name, doc_start, chunks, kv_own, kv_other, after=()):
    _, layers, group, tokens, width = chunks[0].shape
    column_count = len(kv_own)
    merged = len(kv_other) == 1
    block_tokens = kv_own[0].shape[1]
    total = column_count * 2 * block_tokens
    pair = 2 * tokens
    lanes = layers * group * pair
    wide = 2 * pair
    group_lanes = lanes
    while 8 * total * group_lanes > SCORE_BYTES and group_lanes > wide:
        group_lanes = max(k for k in range(wide, group_lanes, wide) if lanes % k == 0)
    smem = pl.BlockSpec(memory_space=pltpu.SMEM)
    vmem = pl.BlockSpec(memory_space=pltpu.VMEM)
    f32, bf16 = jnp.float32, jnp.bfloat16
    outs = [jax.ShapeDtypeStruct((layers, group, tokens, width), bf16)] * 2
    outs.append(jax.ShapeDtypeStruct((column_count, 2, block_tokens, width), f32))
    outs.append(jax.ShapeDtypeStruct((column_count, 2, block_tokens, width), bf16))
    return pl.pallas_call(
        functools.partial(attention_kernel, column_count, group_lanes, merged),
        out_shape=outs,
        in_specs=[smem] + [vmem] * (1 + 2 + column_count + len(kv_other))
        + [pl.BlockSpec(memory_space=pl.ANY)] * len(after),
        out_specs=[vmem] * len(outs),
        scratch_shapes=[
            pltpu.VMEM((layers * group, pair, width), bf16),
            pltpu.VMEM((layers * group, pair, width), bf16),
            pltpu.VMEM((width, lanes), bf16),
            pltpu.VMEM((width, lanes), bf16),
            pltpu.VMEM((total, width), bf16),
            pltpu.VMEM((total, width), bf16),
            pltpu.VMEM((total, group_lanes), f32),
            pltpu.VMEM((total, group_lanes), f32),
            pltpu.VMEM((total // KEY_BLOCK, group_lanes), f32),
            pltpu.VMEM((1, group_lanes), f32),
            pltpu.VMEM((1, group_lanes), f32),
            pltpu.VMEM((1, group_lanes), f32),
            pltpu.VMEM((width, lanes), f32),
            pltpu.VMEM((total, width), f32),
            pltpu.VMEM((total, width), f32),
        ],
        compiler_params=pltpu.CompilerParams(vmem_limit_bytes=VMEM_LIMIT),
        cost_estimate=pl.CostEstimate(
            flops=10 * lanes * total * width,
            bytes_accessed=16 * total * width,
            transcendentals=lanes * total,
        ),
        name=name,
    )(doc_start, doc_start.reshape(-1, pair), *chunks, *kv_own, *kv_other, *after)


def per_device(seq_count, head_count, queries, grad_out, keys, values, doc_start):
    layers, tokens, all_heads, width = queries.shape
    group = all_heads // head_count
    column_count = seq_count // 2
    columns = range(column_count)

    def swap(x, flip_seq, flip_head):
        pairs = [
            (s * head_count + z, (s ^ flip_seq) * head_count + (z ^ flip_head))
            for s in range(seq_count)
            for z in range(head_count)
        ]
        return lax.ppermute(x, ("seq", "head"), pairs)

    z = lax.axis_index("head")

    own = jnp.stack([keys[:, 0], values[:, 0]])
    far_own = swap(own, 0, 2)
    near = [own] + [swap(own, 2 * d, 0) for d in columns[1:]]
    far = [far_own] + [swap(far_own, 2 * d, 0) for d in columns[1:]]
    near_other = [swap(jnp.stack(near), 1, 0)]
    far_other = [swap(x, 1, 0) for x in far]

    both = jnp.stack([queries, grad_out]).reshape(2, layers, tokens, head_count, group, width)
    both = jnp.transpose(both, (3, 0, 1, 4, 2, 5))

    def piece(flip):
        return lax.dynamic_index_in_dim(both, z ^ flip, 0, keepdims=False)

    near_chunks = (piece(0), swap(piece(1), 0, 1))
    far_chunks = (piece(2), swap(piece(3), 0, 1))

    near_dq, near_dq_send, near_kept, near_sent = attention(
        "attention_near", doc_start, near_chunks, near, near_other
    )
    far_dq, far_dq_send, far_kept, far_sent = attention(
        "attention_far", doc_start, far_chunks, far, far_other
    )

    def add_cores(kept, sent):
        sums = kept + swap(sent, 1, 0).astype(jnp.float32)
        return sums[0], [sums[d].astype(jnp.bfloat16) for d in columns[1:]]

    def add_columns(mine, parts):
        for d, part in zip(columns[1:], parts):
            mine = mine + swap(part, 2 * d, 0).astype(jnp.float32)
        return mine

    far_kept_total, far_sent_total = far_kept[0], far_sent[0].astype(jnp.float32)
    for d in columns[1:]:
        both_cores = swap(jnp.stack([far_kept[d].astype(jnp.bfloat16), far_sent[d]]), 2 * d, 0)
        both_cores = both_cores.astype(jnp.float32)
        far_kept_total = far_kept_total + both_cores[0]
        far_sent_total = far_sent_total + both_cores[1]
    far_back, far_sent_low = lax.optimization_barrier(
        (swap(far_dq_send, 0, 1), far_sent_total.astype(jnp.bfloat16))
    )
    far_by_core = swap(far_sent_low, 1, 0)
    far_total = far_kept_total + far_by_core.astype(jnp.float32)
    far_low = far_total.astype(jnp.bfloat16)
    near_sums = add_cores(near_kept, near_sent)
    near_total = add_columns(*near_sums)
    final = near_total + swap(far_low, 0, 2).astype(jnp.float32)
    final = final.astype(jnp.bfloat16)[:, :, None, :]

    near_back, _ = lax.optimization_barrier((swap(near_dq_send, 0, 1), near_sums[1][0]))
    pieces = jnp.stack([near_dq, near_back, far_dq, far_back])
    ordered = [
        lax.dynamic_index_in_dim(pieces, z ^ head, 0, keepdims=False) for head in range(head_count)
    ]
    query_grads = jnp.transpose(jnp.stack(ordered), (1, 3, 0, 2, 4))
    query_grads = query_grads.reshape(layers, tokens, all_heads, width)
    return query_grads, final[0], final[1]


def solution(mesh):
    tokens_spec = P(None, ("seq", "head"), None, None)
    keys_spec = P("seq", "head", None)
    return jax.shard_map(
        functools.partial(per_device, mesh.shape["seq"], mesh.shape["head"]),
        mesh=mesh,
        in_specs=(tokens_spec, tokens_spec, keys_spec, keys_spec, P()),
        out_specs=(tokens_spec, keys_spec, keys_spec),
        check_vma=False,
    )
```

```python
import functools
import math

import jax
import jax.numpy as jnp
from jax import lax
from jax.experimental import pallas as pl
from jax.experimental.pallas import tpu as pltpu
from jax.sharding import PartitionSpec as P

NEG = -1e30
KEY_BLOCK = 256
VMEM_LIMIT = 48 * 1024 * 1024
SCORE_BYTES = 24 * 1024 * 1024


def attention_kernel(column_count, group_lanes, merged, doc_ref, doc_rows_ref, *refs):
    chunk_refs = refs[:2]
    kv_refs = refs[2 : 2 + column_count]
    kv_other = refs[2 + column_count : 2 + 2 * column_count]
    if merged:
        kv_other = [refs[2 + column_count].at[d] for d in range(column_count)]
    (
        dq_own, dq_send, kept_ref, sent_ref,
        q_rows, g_rows, q_cols, g_cols, keys, values,
        e_scr, d_scr, m_scr, max_scr, sum_scr, weight_scr, dqt, dk_acc, dv_acc,
    ) = refs[-19:]
    layers, group, tokens, width = dq_own.shape
    block_tokens = kv_refs[0].shape[1]
    pair = 2 * tokens
    heads = layers * group
    lanes = heads * pair
    wide = 2 * pair
    scale = 1.0 / math.sqrt(width)
    exp_scale = scale * math.log2(math.e)
    s = lax.axis_index("seq")
    z = lax.axis_index("head")
    column, core, z_pair, z_bit = s // 2, s % 2, z // 2, z % 2

    first = (column * 2 + core) * block_tokens + z_pair * pair
    last = first + pair - 1
    low = doc_ref[first] // KEY_BLOCK
    high = last // KEY_BLOCK + 1
    open_from = doc_ref[last]
    starts = doc_rows_ref[pl.ds(first // pair, 1), :]
    places = first + lax.broadcasted_iota(jnp.int32, (1, pair), 1)

    for d in range(column_count):
        for b in range(2):
            start = pl.multiple_of(((column ^ d) * 2 + (core ^ b)) * block_tokens, block_tokens)

            @pl.when((start <= last) & (start + block_tokens > low * KEY_BLOCK))
            def _():
                block = kv_other[d] if b else kv_refs[d]
                keys[pl.ds(start, block_tokens), :] = block[0]
                values[pl.ds(start, block_tokens), :] = block[1]

    if group_lanes != lanes:
        dk_acc[...] = jnp.zeros_like(dk_acc)
        dv_acc[...] = jnp.zeros_like(dv_acc)
    for layer in range(layers):
        for h in range(group):
            n = layer * group + h
            for dz in range(2):
                at = pl.multiple_of((z_bit ^ dz) * tokens, tokens)
                q_rows[n, pl.ds(at, tokens), :] = chunk_refs[dz][0, layer, h]
                g_rows[n, pl.ds(at, tokens), :] = chunk_refs[dz][1, layer, h]
            q_cols[:, n * pair : (n + 1) * pair] = q_rows[n].T
            g_cols[:, n * pair : (n + 1) * pair] = g_rows[n].T

    def over_keys(step):
        count = high - low

        def four(i, _):
            step(low + 4 * i, 4 * KEY_BLOCK)
            return 0

        lax.fori_loop(0, count // 4, four, 0)

        @pl.when(count % 4 >= 2)
        def _():
            step(low + count // 4 * 4, 2 * KEY_BLOCK)

        @pl.when(count % 2 == 1)
        def _():
            step(high - 1, KEY_BLOCK)

    for left in range(0, lanes, group_lanes):
        max_scr[...] = jnp.full_like(max_scr, NEG)
        sum_scr[...] = jnp.zeros_like(sum_scr)
        weight_scr[...] = jnp.zeros_like(weight_scr)

        def stats(j, size):
            key_start = pl.multiple_of(j * KEY_BLOCK, KEY_BLOCK)
            rows = pl.ds(key_start, size)
            key_block = keys[rows, :]
            value_block = values[rows, :]

            def run(masked):
                if masked:
                    at = key_start + lax.broadcasted_iota(jnp.int32, (size, pair), 0)
                    allowed = (at >= starts) & (at <= places)
                    allowed = jnp.concatenate([allowed, allowed], axis=1)
                news = []
                for base in range(0, group_lanes, wide):
                    cols = slice(base, base + wide)
                    from_cols = slice(left + base, left + base + wide)
                    scores = jnp.dot(
                        key_block, q_cols[:, from_cols], preferred_element_type=jnp.float32
                    )
                    if masked:
                        scores = jnp.where(allowed, scores, NEG)
                    e_scr[rows, cols] = scores
                    news.append(jnp.maximum(max_scr[:, cols], jnp.max(scores, axis=0, keepdims=True)))
                for base in range(0, group_lanes, wide):
                    cols = slice(base, base + wide)
                    from_cols = slice(left + base, left + base + wide)
                    grads = jnp.dot(
                        value_block, g_cols[:, from_cols], preferred_element_type=jnp.float32
                    )
                    old, new = max_scr[:, cols], news[base // wide]
                    weights = jnp.exp2((e_scr[rows, cols] - new) * exp_scale)
                    rescale = jnp.exp2((old - new) * exp_scale)
                    max_scr[:, cols] = new
                    m_scr[pl.ds(j, 1), cols] = new
                    sum_scr[:, cols] = sum_scr[:, cols] * rescale + jnp.sum(
                        weights, axis=0, keepdims=True
                    )
                    weight_scr[:, cols] = weight_scr[:, cols] * rescale + jnp.sum(
                        weights * grads, axis=0, keepdims=True
                    )
                    e_scr[rows, cols] = weights
                    d_scr[rows, cols] = grads

            whole = (key_start + size - 1 <= first) & (key_start >= open_from)

            @pl.when(whole)
            def _():
                run(False)

            @pl.when(jnp.logical_not(whole))
            def _():
                run(True)

        over_keys(stats)
        inverse = 1.0 / sum_scr[...]
        weight_scr[...] = weight_scr[...] * inverse
        sum_scr[...] = inverse
        here = slice(left, left + group_lanes)
        dqt[:, here] = jnp.zeros((width, group_lanes), jnp.float32)

        def grads_step(j, size):
            key_start = pl.multiple_of(j * KEY_BLOCK, KEY_BLOCK)
            rows = pl.ds(key_start, size)
            factor = jnp.exp2((m_scr[pl.ds(j, 1), :] - max_scr[...]) * exp_scale) * sum_scr[...]
            probs_parts, grad_parts = [], []
            for base in range(0, group_lanes, wide):
                cols = slice(base, base + wide)
                probs = e_scr[rows, cols] * factor[:, cols]
                grad_scores = probs * (d_scr[rows, cols] - weight_scr[:, cols])
                probs_parts.append(probs.astype(jnp.bfloat16))
                grad_parts.append(grad_scores.astype(jnp.bfloat16))
            probs_low = jnp.concatenate(probs_parts, axis=1)
            grad_low = jnp.concatenate(grad_parts, axis=1)
            mine = slice(left // pair, (left + group_lanes) // pair)
            g_all = g_rows[mine].reshape(group_lanes, width)
            q_all = q_rows[mine].reshape(group_lanes, width)
            dv_part = jnp.dot(probs_low, g_all, preferred_element_type=jnp.float32)
            dk_part = jnp.dot(grad_low, q_all, preferred_element_type=jnp.float32)
            if group_lanes == lanes:
                dv_acc[rows, :] = dv_part
                dk_acc[rows, :] = dk_part
            else:
                dv_acc[rows, :] += dv_part
                dk_acc[rows, :] += dk_part
            dqt[:, here] += jnp.dot(keys[rows, :].T, grad_low, preferred_element_type=jnp.float32)

        over_keys(grads_step)

    for n in range(heads):
        q_rows[n] = (dqt[:, n * pair : (n + 1) * pair] * scale).T.astype(jnp.bfloat16)
        for dz, out in enumerate((dq_own, dq_send)):
            at = pl.multiple_of((z_bit ^ dz) * tokens, tokens)
            out[n // group, n % group] = q_rows[n, pl.ds(at, tokens), :]

    for d in range(column_count):
        for b, out in enumerate((kept_ref, sent_ref)):
            start = pl.multiple_of(((column ^ d) * 2 + (core ^ b)) * block_tokens, block_tokens)
            rows = pl.ds(start, block_tokens)
            seen = (start >= low * KEY_BLOCK) & (start < high * KEY_BLOCK)

            @pl.when(seen)
            def _():
                out[d, 0] = (dk_acc[rows, :] * scale).astype(out.dtype)
                out[d, 1] = dv_acc[rows, :].astype(out.dtype)

            @pl.when(jnp.logical_not(seen))
            def _():
                out[d] = jnp.zeros(out.shape[1:], out.dtype)


def attention(name, doc_start, chunks, kv_own, kv_other, after=()):
    _, layers, group, tokens, width = chunks[0].shape
    column_count = len(kv_own)
    merged = len(kv_other) == 1
    block_tokens = kv_own[0].shape[1]
    total = column_count * 2 * block_tokens
    pair = 2 * tokens
    lanes = layers * group * pair
    wide = 2 * pair
    group_lanes = lanes
    while 8 * total * group_lanes > SCORE_BYTES and group_lanes > wide:
        group_lanes = max(k for k in range(wide, group_lanes, wide) if lanes % k == 0)
    smem = pl.BlockSpec(memory_space=pltpu.SMEM)
    vmem = pl.BlockSpec(memory_space=pltpu.VMEM)
    f32, bf16 = jnp.float32, jnp.bfloat16
    outs = [jax.ShapeDtypeStruct((layers, group, tokens, width), bf16)] * 2
    outs.append(jax.ShapeDtypeStruct((column_count, 2, block_tokens, width), f32))
    outs.append(jax.ShapeDtypeStruct((column_count, 2, block_tokens, width), bf16))
    return pl.pallas_call(
        functools.partial(attention_kernel, column_count, group_lanes, merged),
        out_shape=outs,
        in_specs=[smem] + [vmem] * (1 + 2 + column_count + len(kv_other))
        + [pl.BlockSpec(memory_space=pl.ANY)] * len(after),
        out_specs=[vmem] * len(outs),
        scratch_shapes=[
            pltpu.VMEM((layers * group, pair, width), bf16),
            pltpu.VMEM((layers * group, pair, width), bf16),
            pltpu.VMEM((width, lanes), bf16),
            pltpu.VMEM((width, lanes), bf16),
            pltpu.VMEM((total, width), bf16),
            pltpu.VMEM((total, width), bf16),
            pltpu.VMEM((total, group_lanes), f32),
            pltpu.VMEM((total, group_lanes), f32),
            pltpu.VMEM((total // KEY_BLOCK, group_lanes), f32),
            pltpu.VMEM((1, group_lanes), f32),
            pltpu.VMEM((1, group_lanes), f32),
            pltpu.VMEM((1, group_lanes), f32),
            pltpu.VMEM((width, lanes), f32),
            pltpu.VMEM((total, width), f32),
            pltpu.VMEM((total, width), f32),
        ],
        compiler_params=pltpu.CompilerParams(vmem_limit_bytes=VMEM_LIMIT),
        cost_estimate=pl.CostEstimate(
            flops=10 * lanes * total * width,
            bytes_accessed=16 * total * width,
            transcendentals=lanes * total,
        ),
        name=name,
    )(doc_start, doc_start.reshape(-1, pair), *chunks, *kv_own, *kv_other, *after)


def per_device(seq_count, head_count, queries, grad_out, keys, values, doc_start):
    layers, tokens, all_heads, width = queries.shape
    group = all_heads // head_count
    column_count = seq_count // 2
    columns = range(column_count)

    def swap(x, flip_seq, flip_head):
        pairs = [
            (s * head_count + z, (s ^ flip_seq) * head_count + (z ^ flip_head))
            for s in range(seq_count)
            for z in range(head_count)
        ]
        return lax.ppermute(x, ("seq", "head"), pairs)

    z = lax.axis_index("head")

    own = jnp.stack([keys[:, 0], values[:, 0]])
    far_own = swap(own, 0, 2)
    near = [own] + [swap(own, 2 * d, 0) for d in columns[1:]]
    far = [far_own] + [swap(far_own, 2 * d, 0) for d in columns[1:]]
    near_other = [swap(jnp.stack(near), 1, 0)]
    far_other = [swap(x, 1, 0) for x in far]

    both = jnp.stack([queries, grad_out]).reshape(2, layers, tokens, head_count, group, width)
    both = jnp.transpose(both, (3, 0, 1, 4, 2, 5))

    def piece(flip):
        return lax.dynamic_index_in_dim(both, z ^ flip, 0, keepdims=False)

    far_chunks = (piece(2), swap(piece(3), 0, 1))
    near_chunks = (piece(0), swap(piece(1), 0, 1))

    near_dq, near_dq_send, near_kept, near_sent = attention(
        "attention_near", doc_start, near_chunks, near, near_other
    )
    far_dq, far_dq_send, far_kept, far_sent = attention(
        "attention_far", doc_start, far_chunks, far, far_other
    )

    def add_cores(kept, sent):
        sums = kept + swap(sent, 1, 0).astype(jnp.float32)
        return sums[0], [sums[d].astype(jnp.bfloat16) for d in columns[1:]]

    def add_columns(mine, parts):
        for d, part in zip(columns[1:], parts):
            mine = mine + swap(part, 2 * d, 0).astype(jnp.float32)
        return mine

    far_kept_total, far_sent_total = far_kept[0], far_sent[0].astype(jnp.float32)
    for d in columns[1:]:
        both_cores = swap(jnp.stack([far_kept[d].astype(jnp.bfloat16), far_sent[d]]), 2 * d, 0)
        both_cores = both_cores.astype(jnp.float32)
        far_kept_total = far_kept_total + both_cores[0]
        far_sent_total = far_sent_total + both_cores[1]
    far_back, far_sent_low = lax.optimization_barrier(
        (swap(far_dq_send, 0, 1), far_sent_total.astype(jnp.bfloat16))
    )
    far_by_core = swap(far_sent_low, 1, 0)
    far_total = far_kept_total + far_by_core.astype(jnp.float32)
    far_low = far_total.astype(jnp.bfloat16)
    near_sums = add_cores(near_kept, near_sent)
    near_total = add_columns(*near_sums)
    final = near_total + swap(far_low, 0, 2).astype(jnp.float32)
    final = final.astype(jnp.bfloat16)[:, :, None, :]

    near_back, _ = lax.optimization_barrier((swap(near_dq_send, 0, 1), near_sums[1][0]))
    pieces = jnp.stack([near_dq, near_back, far_dq, far_back])
    ordered = [
        lax.dynamic_index_in_dim(pieces, z ^ head, 0, keepdims=False) for head in range(head_count)
    ]
    query_grads = jnp.transpose(jnp.stack(ordered), (1, 3, 0, 2, 4))
    query_grads = query_grads.reshape(layers, tokens, all_heads, width)
    return query_grads, final[0], final[1]


def solution(mesh):
    tokens_spec = P(None, ("seq", "head"), None, None)
    keys_spec = P("seq", "head", None)
    return jax.shard_map(
        functools.partial(per_device, mesh.shape["seq"], mesh.shape["head"]),
        mesh=mesh,
        in_specs=(tokens_spec, tokens_spec, keys_spec, keys_spec, P()),
        out_specs=(tokens_spec, keys_spec, keys_spec),
        check_vma=False,
    )
```

```python
import functools
import math

import jax
import jax.numpy as jnp
from jax import lax
from jax.experimental import pallas as pl
from jax.experimental.pallas import tpu as pltpu
from jax.sharding import PartitionSpec as P

NEG = -1e30
KEY_BLOCK = 256
VMEM_LIMIT = 48 * 1024 * 1024
SCORE_BYTES = 24 * 1024 * 1024


def attention_kernel(column_count, group_lanes, merged, doc_ref, doc_rows_ref, *refs):
    chunk_refs = refs[:2]
    kv_refs = refs[2 : 2 + column_count]
    kv_other = refs[2 + column_count : 2 + 2 * column_count]
    if merged:
        kv_other = [refs[2 + column_count].at[d] for d in range(column_count)]
    (
        dq_own, dq_send, kept_ref, sent_ref,
        q_rows, g_rows, q_cols, g_cols, keys, values,
        e_scr, d_scr, m_scr, max_scr, sum_scr, weight_scr, dqt, dk_acc, dv_acc,
    ) = refs[-19:]
    layers, group, tokens, width = dq_own.shape
    block_tokens = kv_refs[0].shape[1]
    pair = 2 * tokens
    heads = layers * group
    lanes = heads * pair
    wide = 2 * pair
    scale = 1.0 / math.sqrt(width)
    exp_scale = scale * math.log2(math.e)
    s = lax.axis_index("seq")
    z = lax.axis_index("head")
    column, core, z_pair, z_bit = s // 2, s % 2, z // 2, z % 2

    first = (column * 2 + core) * block_tokens + z_pair * pair
    last = first + pair - 1
    low = doc_ref[first] // KEY_BLOCK
    high = last // KEY_BLOCK + 1
    open_from = doc_ref[last]
    starts = doc_rows_ref[pl.ds(first // pair, 1), :]
    places = first + lax.broadcasted_iota(jnp.int32, (1, pair), 1)

    for d in range(column_count):
        for b in range(2):
            start = pl.multiple_of(((column ^ d) * 2 + (core ^ b)) * block_tokens, block_tokens)

            @pl.when((start <= last) & (start + block_tokens > low * KEY_BLOCK))
            def _():
                block = kv_other[d] if b else kv_refs[d]
                keys[pl.ds(start, block_tokens), :] = block[0]
                values[pl.ds(start, block_tokens), :] = block[1]

    if group_lanes != lanes:
        dk_acc[...] = jnp.zeros_like(dk_acc)
        dv_acc[...] = jnp.zeros_like(dv_acc)
    for layer in range(layers):
        for h in range(group):
            n = layer * group + h
            for dz in range(2):
                at = pl.multiple_of((z_bit ^ dz) * tokens, tokens)
                q_rows[n, pl.ds(at, tokens), :] = chunk_refs[dz][0, layer, h]
                g_rows[n, pl.ds(at, tokens), :] = chunk_refs[dz][1, layer, h]
            q_cols[:, n * pair : (n + 1) * pair] = q_rows[n].T
            g_cols[:, n * pair : (n + 1) * pair] = g_rows[n].T

    def over_keys(step):
        count = high - low

        def four(i, _):
            step(low + 4 * i, 4 * KEY_BLOCK)
            return 0

        lax.fori_loop(0, count // 4, four, 0)

        @pl.when(count % 4 >= 2)
        def _():
            step(low + count // 4 * 4, 2 * KEY_BLOCK)

        @pl.when(count % 2 == 1)
        def _():
            step(high - 1, KEY_BLOCK)

    for left in range(0, lanes, group_lanes):
        max_scr[...] = jnp.full_like(max_scr, NEG)
        sum_scr[...] = jnp.zeros_like(sum_scr)
        weight_scr[...] = jnp.zeros_like(weight_scr)

        def stats(j, size):
            key_start = pl.multiple_of(j * KEY_BLOCK, KEY_BLOCK)
            rows = pl.ds(key_start, size)
            key_block = keys[rows, :]
            value_block = values[rows, :]

            def run(masked):
                if masked:
                    at = key_start + lax.broadcasted_iota(jnp.int32, (size, pair), 0)
                    allowed = (at >= starts) & (at <= places)
                    allowed = jnp.concatenate([allowed, allowed], axis=1)
                news = []
                for base in range(0, group_lanes, wide):
                    cols = slice(base, base + wide)
                    from_cols = slice(left + base, left + base + wide)
                    scores = jnp.dot(
                        key_block, q_cols[:, from_cols], preferred_element_type=jnp.float32
                    )
                    if masked:
                        scores = jnp.where(allowed, scores, NEG)
                    e_scr[rows, cols] = scores
                    news.append(jnp.maximum(max_scr[:, cols], jnp.max(scores, axis=0, keepdims=True)))
                for base in range(0, group_lanes, wide):
                    cols = slice(base, base + wide)
                    from_cols = slice(left + base, left + base + wide)
                    grads = jnp.dot(
                        value_block, g_cols[:, from_cols], preferred_element_type=jnp.float32
                    )
                    old, new = max_scr[:, cols], news[base // wide]
                    weights = jnp.exp2((e_scr[rows, cols] - new) * exp_scale)
                    rescale = jnp.exp2((old - new) * exp_scale)
                    max_scr[:, cols] = new
                    m_scr[pl.ds(j, 1), cols] = new
                    sum_scr[:, cols] = sum_scr[:, cols] * rescale + jnp.sum(
                        weights, axis=0, keepdims=True
                    )
                    weight_scr[:, cols] = weight_scr[:, cols] * rescale + jnp.sum(
                        weights * grads, axis=0, keepdims=True
                    )
                    e_scr[rows, cols] = weights
                    d_scr[rows, cols] = grads

            whole = (key_start + size - 1 <= first) & (key_start >= open_from)

            @pl.when(whole)
            def _():
                run(False)

            @pl.when(jnp.logical_not(whole))
            def _():
                run(True)

        over_keys(stats)
        inverse = 1.0 / sum_scr[...]
        weight_scr[...] = weight_scr[...] * inverse
        sum_scr[...] = inverse
        here = slice(left, left + group_lanes)
        dqt[:, here] = jnp.zeros((width, group_lanes), jnp.float32)

        def grads_step(j, size):
            key_start = pl.multiple_of(j * KEY_BLOCK, KEY_BLOCK)
            rows = pl.ds(key_start, size)
            factor = jnp.exp2((m_scr[pl.ds(j, 1), :] - max_scr[...]) * exp_scale) * sum_scr[...]
            probs_parts, grad_parts = [], []
            for base in range(0, group_lanes, wide):
                cols = slice(base, base + wide)
                probs = e_scr[rows, cols] * factor[:, cols]
                grad_scores = probs * (d_scr[rows, cols] - weight_scr[:, cols])
                probs_parts.append(probs.astype(jnp.bfloat16))
                grad_parts.append(grad_scores.astype(jnp.bfloat16))
            probs_low = jnp.concatenate(probs_parts, axis=1)
            grad_low = jnp.concatenate(grad_parts, axis=1)
            mine = slice(left // pair, (left + group_lanes) // pair)
            g_all = g_rows[mine].reshape(group_lanes, width)
            q_all = q_rows[mine].reshape(group_lanes, width)
            dv_part = jnp.dot(probs_low, g_all, preferred_element_type=jnp.float32)
            dk_part = jnp.dot(grad_low, q_all, preferred_element_type=jnp.float32)
            if group_lanes == lanes:
                dv_acc[rows, :] = dv_part
                dk_acc[rows, :] = dk_part
            else:
                dv_acc[rows, :] += dv_part
                dk_acc[rows, :] += dk_part
            dqt[:, here] += jnp.dot(keys[rows, :].T, grad_low, preferred_element_type=jnp.float32)

        over_keys(grads_step)

    for n in range(heads):
        q_rows[n] = (dqt[:, n * pair : (n + 1) * pair] * scale).T.astype(jnp.bfloat16)
        for dz, out in enumerate((dq_own, dq_send)):
            at = pl.multiple_of((z_bit ^ dz) * tokens, tokens)
            out[n // group, n % group] = q_rows[n, pl.ds(at, tokens), :]

    for d in range(column_count):
        for b, out in enumerate((kept_ref, sent_ref)):
            start = pl.multiple_of(((column ^ d) * 2 + (core ^ b)) * block_tokens, block_tokens)
            rows = pl.ds(start, block_tokens)
            seen = (start >= low * KEY_BLOCK) & (start < high * KEY_BLOCK)

            @pl.when(seen)
            def _():
                out[d, 0] = (dk_acc[rows, :] * scale).astype(out.dtype)
                out[d, 1] = dv_acc[rows, :].astype(out.dtype)

            @pl.when(jnp.logical_not(seen))
            def _():
                out[d] = jnp.zeros(out.shape[1:], out.dtype)


def attention(name, doc_start, chunks, kv_own, kv_other, after=()):
    _, layers, group, tokens, width = chunks[0].shape
    column_count = len(kv_own)
    merged = len(kv_other) == 1
    block_tokens = kv_own[0].shape[1]
    total = column_count * 2 * block_tokens
    pair = 2 * tokens
    lanes = layers * group * pair
    wide = 2 * pair
    group_lanes = lanes
    while 8 * total * group_lanes > SCORE_BYTES and group_lanes > wide:
        group_lanes = max(k for k in range(wide, group_lanes, wide) if lanes % k == 0)
    smem = pl.BlockSpec(memory_space=pltpu.SMEM)
    vmem = pl.BlockSpec(memory_space=pltpu.VMEM)
    f32, bf16 = jnp.float32, jnp.bfloat16
    outs = [jax.ShapeDtypeStruct((layers, group, tokens, width), bf16)] * 2
    outs.append(jax.ShapeDtypeStruct((column_count, 2, block_tokens, width), f32))
    outs.append(jax.ShapeDtypeStruct((column_count, 2, block_tokens, width), bf16))
    return pl.pallas_call(
        functools.partial(attention_kernel, column_count, group_lanes, merged),
        out_shape=outs,
        in_specs=[smem] + [vmem] * (1 + 2 + column_count + len(kv_other))
        + [pl.BlockSpec(memory_space=pl.ANY)] * len(after),
        out_specs=[vmem] * len(outs),
        scratch_shapes=[
            pltpu.VMEM((layers * group, pair, width), bf16),
            pltpu.VMEM((layers * group, pair, width), bf16),
            pltpu.VMEM((width, lanes), bf16),
            pltpu.VMEM((width, lanes), bf16),
            pltpu.VMEM((total, width), bf16),
            pltpu.VMEM((total, width), bf16),
            pltpu.VMEM((total, group_lanes), f32),
            pltpu.VMEM((total, group_lanes), f32),
            pltpu.VMEM((total // KEY_BLOCK, group_lanes), f32),
            pltpu.VMEM((1, group_lanes), f32),
            pltpu.VMEM((1, group_lanes), f32),
            pltpu.VMEM((1, group_lanes), f32),
            pltpu.VMEM((width, lanes), f32),
            pltpu.VMEM((total, width), f32),
            pltpu.VMEM((total, width), f32),
        ],
        compiler_params=pltpu.CompilerParams(vmem_limit_bytes=VMEM_LIMIT),
        cost_estimate=pl.CostEstimate(
            flops=10 * lanes * total * width,
            bytes_accessed=16 * total * width,
            transcendentals=lanes * total,
        ),
        name=name,
    )(doc_start, doc_start.reshape(-1, pair), *chunks, *kv_own, *kv_other, *after)


def per_device(seq_count, head_count, queries, grad_out, keys, values, doc_start):
    layers, tokens, all_heads, width = queries.shape
    group = all_heads // head_count
    column_count = seq_count // 2
    columns = range(column_count)

    def swap(x, flip_seq, flip_head):
        pairs = [
            (s * head_count + z, (s ^ flip_seq) * head_count + (z ^ flip_head))
            for s in range(seq_count)
            for z in range(head_count)
        ]
        return lax.ppermute(x, ("seq", "head"), pairs)

    z = lax.axis_index("head")

    own = jnp.stack([keys[:, 0], values[:, 0]])
    far_own = swap(own, 0, 2)
    near = [own] + [swap(own, 2 * d, 0) for d in columns[1:]]
    far = [far_own] + [swap(far_own, 2 * d, 0) for d in columns[1:]]
    near_other = [swap(jnp.stack(near), 1, 0)]
    far_other = [swap(x, 1, 0) for x in far]

    both = jnp.stack([queries, grad_out]).reshape(2, layers, tokens, head_count, group, width)
    both = jnp.transpose(both, (3, 0, 1, 4, 2, 5))

    def piece(flip):
        return lax.dynamic_index_in_dim(both, z ^ flip, 0, keepdims=False)

    far_chunks = (piece(2), swap(piece(3), 0, 1))
    near_chunks = (piece(0), swap(piece(1), 0, 1))

    near_dq, near_dq_send, near_kept, near_sent = attention(
        "attention_near", doc_start, near_chunks, near, near_other
    )
    far_dq, far_dq_send, far_kept, far_sent = attention(
        "attention_far", doc_start, far_chunks, far, far_other
    )

    def add_cores(kept, sent):
        sums = kept + swap(sent, 1, 0).astype(jnp.float32)
        return sums[0], [sums[d].astype(jnp.bfloat16) for d in columns[1:]]

    def add_columns(mine, parts):
        for d, part in reversed(list(zip(columns[1:], parts))):
            mine = mine + swap(part, 2 * d, 0).astype(jnp.float32)
        return mine

    far_kept_total, far_sent_total = far_kept[0], far_sent[0].astype(jnp.float32)
    for d in reversed(columns[1:]):
        both_cores = swap(jnp.stack([far_kept[d].astype(jnp.bfloat16), far_sent[d]]), 2 * d, 0)
        both_cores = both_cores.astype(jnp.float32)
        far_kept_total = far_kept_total + both_cores[0]
        far_sent_total = far_sent_total + both_cores[1]
    far_back, far_sent_low = lax.optimization_barrier(
        (swap(far_dq_send, 0, 1), far_sent_total.astype(jnp.bfloat16))
    )
    far_by_core = swap(far_sent_low, 1, 0)
    far_total = far_kept_total + far_by_core.astype(jnp.float32)
    far_low = far_total.astype(jnp.bfloat16)
    near_sums = add_cores(near_kept, near_sent)
    near_total = add_columns(*near_sums)
    final = near_total + swap(far_low, 0, 2).astype(jnp.float32)
    final = final.astype(jnp.bfloat16)[:, :, None, :]

    near_back, _ = lax.optimization_barrier((swap(near_dq_send, 0, 1), near_sums[1][0]))
    pieces = jnp.stack([near_dq, near_back, far_dq, far_back])
    ordered = [
        lax.dynamic_index_in_dim(pieces, z ^ head, 0, keepdims=False) for head in range(head_count)
    ]
    query_grads = jnp.transpose(jnp.stack(ordered), (1, 3, 0, 2, 4))
    query_grads = query_grads.reshape(layers, tokens, all_heads, width)
    return query_grads, final[0], final[1]


def solution(mesh):
    tokens_spec = P(None, ("seq", "head"), None, None)
    keys_spec = P("seq", "head", None)
    return jax.shard_map(
        functools.partial(per_device, mesh.shape["seq"], mesh.shape["head"]),
        mesh=mesh,
        in_specs=(tokens_spec, tokens_spec, keys_spec, keys_spec, P()),
        out_specs=(tokens_spec, keys_spec, keys_spec),
        check_vma=False,
    )
```

```python
import functools
import math

import jax
import jax.numpy as jnp
from jax import lax
from jax.experimental import pallas as pl
from jax.experimental.pallas import tpu as pltpu
from jax.sharding import PartitionSpec as P

NEG = -1e30
KEY_BLOCK = 256
VMEM_LIMIT = 48 * 1024 * 1024
SCORE_BYTES = 24 * 1024 * 1024


def attention_kernel(column_count, group_lanes, merged, direct, doc_ref, doc_rows_ref, *refs):
    chunk_refs = refs[:2]
    kv_refs = refs[2 : 2 + column_count]
    kv_other = refs[2 + column_count : 2 + 2 * column_count]
    if merged:
        kv_other = [refs[2 + column_count].at[d] for d in range(column_count)]
    part_count = column_count - 1 if direct else 0
    dq_own, dq_send, kept_ref, sent_ref = refs[-19 - part_count : -15 - part_count]
    part_refs = refs[-15 - part_count : -15]
    (
        q_rows, g_rows, q_cols, g_cols, keys, values,
        e_scr, d_scr, m_scr, max_scr, sum_scr, weight_scr, dqt, dk_acc, dv_acc,
    ) = refs[-15:]
    layers, group, tokens, width = dq_own.shape
    block_tokens = kv_refs[0].shape[1]
    pair = 2 * tokens
    heads = layers * group
    lanes = heads * pair
    wide = 2 * pair
    scale = 1.0 / math.sqrt(width)
    exp_scale = scale * math.log2(math.e)
    s = lax.axis_index("seq")
    z = lax.axis_index("head")
    column, core, z_pair, z_bit = s // 2, s % 2, z // 2, z % 2

    first = (column * 2 + core) * block_tokens + z_pair * pair
    last = first + pair - 1
    low = doc_ref[first] // KEY_BLOCK
    high = last // KEY_BLOCK + 1
    open_from = doc_ref[last]
    starts = doc_rows_ref[pl.ds(first // pair, 1), :]
    places = first + lax.broadcasted_iota(jnp.int32, (1, pair), 1)

    for d in range(column_count):
        for b in range(2):
            start = pl.multiple_of(((column ^ d) * 2 + (core ^ b)) * block_tokens, block_tokens)

            @pl.when((start <= last) & (start + block_tokens > low * KEY_BLOCK))
            def _():
                block = kv_other[d] if b else kv_refs[d]
                keys[pl.ds(start, block_tokens), :] = block[0]
                values[pl.ds(start, block_tokens), :] = block[1]

    if group_lanes != lanes:
        dk_acc[...] = jnp.zeros_like(dk_acc)
        dv_acc[...] = jnp.zeros_like(dv_acc)
    for layer in range(layers):
        for h in range(group):
            n = layer * group + h
            for dz in range(2):
                at = pl.multiple_of((z_bit ^ dz) * tokens, tokens)
                q_rows[n, pl.ds(at, tokens), :] = chunk_refs[dz][0, layer, h]
                g_rows[n, pl.ds(at, tokens), :] = chunk_refs[dz][1, layer, h]
            q_cols[:, n * pair : (n + 1) * pair] = q_rows[n].T
            g_cols[:, n * pair : (n + 1) * pair] = g_rows[n].T

    def over_keys(step):
        count = high - low

        def four(i, _):
            step(low + 4 * i, 4 * KEY_BLOCK)
            return 0

        lax.fori_loop(0, count // 4, four, 0)

        @pl.when(count % 4 >= 2)
        def _():
            step(low + count // 4 * 4, 2 * KEY_BLOCK)

        @pl.when(count % 2 == 1)
        def _():
            step(high - 1, KEY_BLOCK)

    for left in range(0, lanes, group_lanes):
        max_scr[...] = jnp.full_like(max_scr, NEG)
        sum_scr[...] = jnp.zeros_like(sum_scr)
        weight_scr[...] = jnp.zeros_like(weight_scr)

        def stats(j, size):
            key_start = pl.multiple_of(j * KEY_BLOCK, KEY_BLOCK)
            rows = pl.ds(key_start, size)
            key_block = keys[rows, :]
            value_block = values[rows, :]

            def run(masked):
                if masked:
                    at = key_start + lax.broadcasted_iota(jnp.int32, (size, pair), 0)
                    allowed = (at >= starts) & (at <= places)
                    allowed = jnp.concatenate([allowed, allowed], axis=1)
                news = []
                for base in range(0, group_lanes, wide):
                    cols = slice(base, base + wide)
                    from_cols = slice(left + base, left + base + wide)
                    scores = jnp.dot(
                        key_block, q_cols[:, from_cols], preferred_element_type=jnp.float32
                    )
                    if masked:
                        scores = jnp.where(allowed, scores, NEG)
                    e_scr[rows, cols] = scores
                    news.append(jnp.maximum(max_scr[:, cols], jnp.max(scores, axis=0, keepdims=True)))
                for base in range(0, group_lanes, wide):
                    cols = slice(base, base + wide)
                    from_cols = slice(left + base, left + base + wide)
                    grads = jnp.dot(
                        value_block, g_cols[:, from_cols], preferred_element_type=jnp.float32
                    )
                    old, new = max_scr[:, cols], news[base // wide]
                    weights = jnp.exp2((e_scr[rows, cols] - new) * exp_scale)
                    rescale = jnp.exp2((old - new) * exp_scale)
                    max_scr[:, cols] = new
                    m_scr[pl.ds(j, 1), cols] = new
                    sum_scr[:, cols] = sum_scr[:, cols] * rescale + jnp.sum(
                        weights, axis=0, keepdims=True
                    )
                    weight_scr[:, cols] = weight_scr[:, cols] * rescale + jnp.sum(
                        weights * grads, axis=0, keepdims=True
                    )
                    e_scr[rows, cols] = weights
                    d_scr[rows, cols] = grads

            whole = (key_start + size - 1 <= first) & (key_start >= open_from)

            @pl.when(whole)
            def _():
                run(False)

            @pl.when(jnp.logical_not(whole))
            def _():
                run(True)

        over_keys(stats)
        inverse = 1.0 / sum_scr[...]
        weight_scr[...] = weight_scr[...] * inverse
        sum_scr[...] = inverse
        here = slice(left, left + group_lanes)
        dqt[:, here] = jnp.zeros((width, group_lanes), jnp.float32)

        def grads_step(j, size):
            key_start = pl.multiple_of(j * KEY_BLOCK, KEY_BLOCK)
            rows = pl.ds(key_start, size)
            factor = jnp.exp2((m_scr[pl.ds(j, 1), :] - max_scr[...]) * exp_scale) * sum_scr[...]
            probs_parts, grad_parts = [], []
            for base in range(0, group_lanes, wide):
                cols = slice(base, base + wide)
                probs = e_scr[rows, cols] * factor[:, cols]
                grad_scores = probs * (d_scr[rows, cols] - weight_scr[:, cols])
                probs_parts.append(probs.astype(jnp.bfloat16))
                grad_parts.append(grad_scores.astype(jnp.bfloat16))
            probs_low = jnp.concatenate(probs_parts, axis=1)
            grad_low = jnp.concatenate(grad_parts, axis=1)
            mine = slice(left // pair, (left + group_lanes) // pair)
            g_all = g_rows[mine].reshape(group_lanes, width)
            q_all = q_rows[mine].reshape(group_lanes, width)
            dv_part = jnp.dot(probs_low, g_all, preferred_element_type=jnp.float32)
            dk_part = jnp.dot(grad_low, q_all, preferred_element_type=jnp.float32)
            if group_lanes == lanes:
                dv_acc[rows, :] = dv_part
                dk_acc[rows, :] = dk_part
            else:
                dv_acc[rows, :] += dv_part
                dk_acc[rows, :] += dk_part
            dqt[:, here] += jnp.dot(keys[rows, :].T, grad_low, preferred_element_type=jnp.float32)

        over_keys(grads_step)

    for n in range(heads):
        q_rows[n] = (dqt[:, n * pair : (n + 1) * pair] * scale).T.astype(jnp.bfloat16)
        for dz, out in enumerate((dq_own, dq_send)):
            at = pl.multiple_of((z_bit ^ dz) * tokens, tokens)
            out[n // group, n % group] = q_rows[n, pl.ds(at, tokens), :]

    for d in range(column_count):
        for b, near_ref in enumerate((kept_ref, sent_ref)):
            if direct:
                out = part_refs[d - 1].at[b] if d else near_ref
            else:
                out = near_ref.at[d]
            start = pl.multiple_of(((column ^ d) * 2 + (core ^ b)) * block_tokens, block_tokens)
            rows = pl.ds(start, block_tokens)
            seen = (start >= low * KEY_BLOCK) & (start < high * KEY_BLOCK)

            @pl.when(seen)
            def _():
                out[0] = (dk_acc[rows, :] * scale).astype(out.dtype)
                out[1] = dv_acc[rows, :].astype(out.dtype)

            @pl.when(jnp.logical_not(seen))
            def _():
                out[...] = jnp.zeros(out.shape, out.dtype)


def attention(name, doc_start, chunks, kv_own, kv_other, direct=False, after=()):
    _, layers, group, tokens, width = chunks[0].shape
    column_count = len(kv_own)
    merged = len(kv_other) == 1
    block_tokens = kv_own[0].shape[1]
    total = column_count * 2 * block_tokens
    pair = 2 * tokens
    lanes = layers * group * pair
    wide = 2 * pair
    group_lanes = lanes
    while 8 * total * group_lanes > SCORE_BYTES and group_lanes > wide:
        group_lanes = max(k for k in range(wide, group_lanes, wide) if lanes % k == 0)
    smem = pl.BlockSpec(memory_space=pltpu.SMEM)
    vmem = pl.BlockSpec(memory_space=pltpu.VMEM)
    f32, bf16 = jnp.float32, jnp.bfloat16
    outs = [jax.ShapeDtypeStruct((layers, group, tokens, width), bf16)] * 2
    block = (2, block_tokens, width)
    if direct:
        outs += [jax.ShapeDtypeStruct(block, f32), jax.ShapeDtypeStruct(block, bf16)]
        outs += [jax.ShapeDtypeStruct((2,) + block, bf16)] * (column_count - 1)
    else:
        outs.append(jax.ShapeDtypeStruct((column_count,) + block, f32))
        outs.append(jax.ShapeDtypeStruct((column_count,) + block, bf16))
    return pl.pallas_call(
        functools.partial(attention_kernel, column_count, group_lanes, merged, direct),
        out_shape=outs,
        in_specs=[smem] + [vmem] * (1 + 2 + column_count + len(kv_other))
        + [pl.BlockSpec(memory_space=pl.ANY)] * len(after),
        out_specs=[vmem] * len(outs),
        scratch_shapes=[
            pltpu.VMEM((layers * group, pair, width), bf16),
            pltpu.VMEM((layers * group, pair, width), bf16),
            pltpu.VMEM((width, lanes), bf16),
            pltpu.VMEM((width, lanes), bf16),
            pltpu.VMEM((total, width), bf16),
            pltpu.VMEM((total, width), bf16),
            pltpu.VMEM((total, group_lanes), f32),
            pltpu.VMEM((total, group_lanes), f32),
            pltpu.VMEM((total // KEY_BLOCK, group_lanes), f32),
            pltpu.VMEM((1, group_lanes), f32),
            pltpu.VMEM((1, group_lanes), f32),
            pltpu.VMEM((1, group_lanes), f32),
            pltpu.VMEM((width, lanes), f32),
            pltpu.VMEM((total, width), f32),
            pltpu.VMEM((total, width), f32),
        ],
        compiler_params=pltpu.CompilerParams(vmem_limit_bytes=VMEM_LIMIT),
        cost_estimate=pl.CostEstimate(
            flops=10 * lanes * total * width,
            bytes_accessed=16 * total * width,
            transcendentals=lanes * total,
        ),
        name=name,
    )(doc_start, doc_start.reshape(-1, pair), *chunks, *kv_own, *kv_other, *after)


def per_device(seq_count, head_count, queries, grad_out, keys, values, doc_start):
    layers, tokens, all_heads, width = queries.shape
    group = all_heads // head_count
    column_count = seq_count // 2
    columns = range(column_count)

    def swap(x, flip_seq, flip_head):
        pairs = [
            (s * head_count + z, (s ^ flip_seq) * head_count + (z ^ flip_head))
            for s in range(seq_count)
            for z in range(head_count)
        ]
        return lax.ppermute(x, ("seq", "head"), pairs)

    z = lax.axis_index("head")

    own = jnp.stack([keys[:, 0], values[:, 0]])
    far_own = swap(own, 0, 2)
    near = [own] + [swap(own, 2 * d, 0) for d in columns[1:]]
    far = [far_own] + [swap(far_own, 2 * d, 0) for d in columns[1:]]
    near_other = [swap(jnp.stack(near), 1, 0)]
    far_other = [swap(x, 1, 0) for x in far]

    both = jnp.stack([queries, grad_out]).reshape(2, layers, tokens, head_count, group, width)
    both = jnp.transpose(both, (3, 0, 1, 4, 2, 5))

    def piece(flip):
        return lax.dynamic_index_in_dim(both, z ^ flip, 0, keepdims=False)

    far_chunks = (piece(2), swap(piece(3), 0, 1))
    near_chunks = (piece(0), swap(piece(1), 0, 1))

    near_dq, near_dq_send, near_kept, near_sent = attention(
        "attention_near", doc_start, near_chunks, near, near_other
    )
    far_dq, far_dq_send, far_kept, far_sent, *far_parts = attention(
        "attention_far", doc_start, far_chunks, far, far_other, True
    )

    def add_cores(kept, sent):
        sums = kept + swap(sent, 1, 0).astype(jnp.float32)
        return sums[0], [sums[d].astype(jnp.bfloat16) for d in columns[1:]]

    def add_columns(mine, parts):
        for d, part in zip(columns[1:], parts):
            mine = mine + swap(part, 2 * d, 0).astype(jnp.float32)
        return mine

    far_kept_total, far_sent_total = far_kept, far_sent.astype(jnp.float32)
    for d in columns[1:]:
        both_cores = swap(far_parts[d - 1], 2 * d, 0)
        both_cores = both_cores.astype(jnp.float32)
        far_kept_total = far_kept_total + both_cores[0]
        far_sent_total = far_sent_total + both_cores[1]
    far_back, far_sent_low = lax.optimization_barrier(
        (swap(far_dq_send, 0, 1), far_sent_total.astype(jnp.bfloat16))
    )
    far_by_core = swap(far_sent_low, 1, 0)
    far_total = far_kept_total + far_by_core.astype(jnp.float32)
    far_low = far_total.astype(jnp.bfloat16)
    near_sums = add_cores(near_kept, near_sent)
    near_total = add_columns(*near_sums)
    final = near_total + swap(far_low, 0, 2).astype(jnp.float32)
    final = final.astype(jnp.bfloat16)[:, :, None, :]

    near_back, _ = lax.optimization_barrier((swap(near_dq_send, 0, 1), near_sums[1][0]))
    pieces = jnp.stack([near_dq, near_back, far_dq, far_back])
    ordered = [
        lax.dynamic_index_in_dim(pieces, z ^ head, 0, keepdims=False) for head in range(head_count)
    ]
    query_grads = jnp.transpose(jnp.stack(ordered), (1, 3, 0, 2, 4))
    query_grads = query_grads.reshape(layers, tokens, all_heads, width)
    return query_grads, final[0], final[1]


def solution(mesh):
    tokens_spec = P(None, ("seq", "head"), None, None)
    keys_spec = P("seq", "head", None)
    return jax.shard_map(
        functools.partial(per_device, mesh.shape["seq"], mesh.shape["head"]),
        mesh=mesh,
        in_specs=(tokens_spec, tokens_spec, keys_spec, keys_spec, P()),
        out_specs=(tokens_spec, keys_spec, keys_spec),
        check_vma=False,
    )
```
